512 devices in a mesh: seq: 64 (over y_hi, z, core), chan: 8 (over y_lo, x).
Axes of the slice: x: 4, y: 8 (y_hi: 4, y_lo: 2; y = y_hi * 2 + y_lo), z: 8, core: 2. Of those that a mesh axis runs over, the one named last changes fastest.
Arguments:
- queries: float32 [128, 524288], P(None, ('seq', 'chan')), may hold values from -6 to 6
- keys: float32 [128, 524288], P(None, ('seq', 'chan')), may hold values from -6 to 6
- values: float32 [128, 524288], P(None, ('seq', 'chan')), may hold values from -6 to 6
- short_taps: float32 [3, 3, 128], replicated, may hold values from -3 to 3
- long_filter: float32 [128, 524288], P('chan', 'seq'), may hold values from -2 to 2
- skip_gain: float32 [128], replicated, may hold values from 0.5 to 1.5
Outputs:
- gated_output: float32 [128, 524288], P(None, ('seq', 'chan'))
The draws below stay inside these ranges and needn't reach their ends.
All inputs are finite; a program needn't handle non-finite values.
Results may differ from the reference program's by a relative error of at most 0.00016.
Values sent between devices are 32-bit elements; how exact they have to be, the bound alone decides.
No kernel may reach another device: no remote copies, remote signals or barrier semaphores. Data moves between devices by JAX's collectives and lax.ppermute only.
A program may use at most 64 MiB of HBM per device.

```python
import math
import jax
import jax.numpy as jnp
from jax import lax

GROUP_CHANNELS = 128
TAPS = 3
SEQUENCE_LENGTH = 524288


def draw_long_filter(key, part):
    key = jax.random.fold_in(key, 7)
    key_kind, key_slow, key_fast, key_rough, position_key, height_key, share_key, cutoff_key = jax.random.split(key, 8)
    slow_share = 0.5
    rough_part = jnp.clip(jax.random.normal(key_rough, (GROUP_CHANNELS, SEQUENCE_LENGTH), jnp.float32), -4.0, 4.0)
    is_slow = jax.random.uniform(key_kind, (GROUP_CHANNELS, 1), jnp.float32) < slow_share
    share_draw = jax.random.uniform(share_key, (GROUP_CHANNELS, 1), jnp.float32, 0.0, 0.1)
    slow_energy = jnp.where(is_slow, 0.8 + share_draw, 0.2 + share_draw)
    slow_rate = jnp.exp(jax.random.uniform(key_slow, (GROUP_CHANNELS, 1), jnp.float32, math.log(0.1 / SEQUENCE_LENGTH), math.log(1.0 / SEQUENCE_LENGTH)))
    fast_rate = jnp.exp(jax.random.uniform(key_fast, (GROUP_CHANNELS, 1), jnp.float32, math.log(1.0 / 50.0), math.log(1.0 / 30.0)))
    sequence_positions = jnp.arange(SEQUENCE_LENGTH, dtype=jnp.float32)[None, :]
    slow_amplitude = jnp.sqrt(2.0 * slow_rate / (1.0 - jnp.exp(-2.0 * slow_rate * SEQUENCE_LENGTH)))
    fast_amplitude = jnp.sqrt(2.0 * fast_rate / (1.0 - jnp.exp(-2.0 * fast_rate * SEQUENCE_LENGTH)))
    slow_mode = jnp.sqrt(slow_energy) * slow_amplitude * jnp.exp(-slow_rate * sequence_positions)
    fast_mode = jnp.sqrt(1.0 - slow_energy) * fast_amplitude * jnp.exp(-fast_rate * sequence_positions)
    spike_position = jax.random.randint(position_key, (GROUP_CHANNELS, 3), 0, SEQUENCE_LENGTH).astype(jnp.float32)
    spike_height = jax.random.uniform(height_key, (GROUP_CHANNELS, 3), jnp.float32, 0.5, 0.8)
    multiplier = jnp.ones((GROUP_CHANNELS, SEQUENCE_LENGTH), jnp.float32)
    for spike_pulse in range(3):
        multiplier = multiplier * jnp.where(sequence_positions >= spike_position[:, spike_pulse:spike_pulse + 1], spike_height[:, spike_pulse:spike_pulse + 1], 1.0)
    has_cutoff = jax.random.uniform(cutoff_key, (GROUP_CHANNELS, 1), jnp.float32) < 0.25
    cutoff_at = float(SEQUENCE_LENGTH - SEQUENCE_LENGTH // 4)
    support = jnp.where(has_cutoff & (sequence_positions >= cutoff_at), 0.0, 1.0)
    return rough_part * (slow_mode + fast_mode) * multiplier * support


def block_levels(own_key, extent, cuts, low, largest):
    loudness, own = 1.0, jax.random.fold_in(own_key, 6)
    for position, shards_of in cuts:
        draws = jnp.exp(jax.random.uniform(jax.random.fold_in(own, position), (shards_of,), jnp.float32, low / len(cuts), largest / len(cuts)))
        loudness = loudness * jnp.repeat(draws, extent[position] // shards_of).reshape([-1 if axis == position else 1 for axis in range(len(extent))])
    return loudness


def bell_draw(stream_key, shape, spread, bound, cuts=(), kind=jnp.bfloat16):
    loudness = block_levels(stream_key, shape, cuts, -0.22, 0.18) if cuts else 1.0
    values = jax.random.normal(stream_key, shape, jnp.float32) * spread * loudness
    return jnp.minimum(jnp.maximum(values, -bound), bound).astype(kind)


def setup_inputs(seed: int = 0) -> dict:
    key_list = jax.random.split(jax.random.key(seed), 7)
    return {
        "queries": bell_draw(key_list[0], (GROUP_CHANNELS, SEQUENCE_LENGTH), 1.0, 6.0, ((1, 512),), jnp.float32),
        "keys": bell_draw(key_list[1], (GROUP_CHANNELS, SEQUENCE_LENGTH), 1.0, 6.0, ((1, 512),), jnp.float32),
        "values": bell_draw(key_list[2], (GROUP_CHANNELS, SEQUENCE_LENGTH), 1.0, 6.0, ((1, 512),), jnp.float32),
        "short_taps": bell_draw(key_list[3], (3, TAPS, GROUP_CHANNELS), 0.6, 3.0, (), jnp.float32),
        "long_filter": draw_long_filter(jax.random.fold_in(key_list[6], 71), 0),
        "skip_gain": jnp.clip(jax.random.uniform(key_list[5], (GROUP_CHANNELS,), jnp.float32, 0.5, 1.5), 0.5, 1.5),
    }


def causal_short(signal, weights):
    result = weights[0][:, None] * signal
    for offset in range(1, weights.shape[0]):
        delayed = jnp.pad(signal, ((0, 0), (offset, 0)))[:, :-offset]
        result = result + weights[offset][:, None] * delayed
    return result


def reference(queries, keys, values, short_taps, long_filter, skip_gain):
    query_feat = causal_short(queries, short_taps[0])
    key_feat = causal_short(keys, short_taps[1])
    value_feat = causal_short(values, short_taps[2])
    drive_signal = key_feat * value_feat

    def convolve_one(pair):
        signal_row, filter_row = pair
        spectrum = jnp.fft.rfft(signal_row, n=2 * SEQUENCE_LENGTH) * jnp.fft.rfft(filter_row, n=2 * SEQUENCE_LENGTH)
        return jnp.fft.irfft(spectrum, n=2 * SEQUENCE_LENGTH)[:SEQUENCE_LENGTH]

    convolved = lax.map(convolve_one, (drive_signal, long_filter))
    return query_feat * (convolved + skip_gain[:, None] * drive_signal)
```

```python
import functools

import jax
import jax.numpy as jnp
import numpy as np
from jax import lax
from jax.experimental import pallas as pl
from jax.experimental.pallas import tpu as pltpu
from jax.sharding import PartitionSpec as P


BF = jnp.bfloat16
F32 = jnp.float32
GROUP = 4
ROWS = 512
COLS = 1024
QUARTER = COLS // GROUP
MINE = ROWS // GROUP
LANES = 128
TOTAL = ROWS * COLS


def halves(values):
    high = np.asarray(values, np.float32).astype(jnp.bfloat16)
    low = (np.asarray(values, np.float64) - high.astype(np.float64)).astype(np.float32).astype(jnp.bfloat16)
    return high, low


@functools.lru_cache(maxsize=None)
def tables():
    k1 = np.arange(ROWS, dtype=np.float64)[:, None] + 0.25
    p = np.arange(ROWS, dtype=np.float64)[None, :]
    angle = 2.0 * np.pi * k1 * p / ROWS
    cos, sin = np.cos(angle), np.sin(angle)
    outer = np.stack((cos.reshape(GROUP, MINE, ROWS), -sin.reshape(GROUP, MINE, ROWS)), 1).reshape(2 * ROWS, ROWS)
    forward = halves(outer)
    backward = halves(outer.T / TOTAL)
    j = np.arange(COLS, dtype=np.float64)[None, :]
    turn = 2.0 * np.pi * k1 * j / TOTAL
    turns = np.stack((np.cos(turn).reshape(GROUP, MINE, COLS), -np.sin(turn).reshape(GROUP, MINE, COLS)), 1)
    i = np.arange(QUARTER, dtype=np.float64)
    small = 2.0 * np.pi * np.arange(GROUP)[:, None] * i[None, :] / COLS
    steps = np.stack((np.cos(small), -np.sin(small)), 1).reshape(2 * GROUP, QUARTER)
    inner = 2.0 * np.pi * np.outer(i, i) / QUARTER
    inner_high, inner_low = halves(np.concatenate((np.cos(inner), -np.sin(inner)), 1))
    inner3 = np.concatenate((inner_high, inner_high, inner_low), 0)
    return forward, backward, turns.astype(np.float32), steps.astype(np.float32), inner3


def split(x):
    high = x.astype(BF)
    return high, (x - high.astype(F32)).astype(BF)


def mm(a, b):
    return jnp.dot(a, b, preferred_element_type=F32)


def pack_rows(out_ref, chan, values, base):
    for quarter in range(GROUP):
        for half in range(2):
            at = (2 * quarter + half) * LANES
            out_ref[pl.ds(16 * quarter + 2 * chan + half, 16, stride=64), :] = values[:, base + at : base + at + LANES]


def pack_filter_kernel(filter_ref, out_ref):
    for chan in range(8):
        pack_rows(out_ref, chan, filter_ref[:, chan * COLS : (chan + 1) * COLS], 0)


def feature(signal, taps, older, newer):
    lane = lax.broadcasted_iota(jnp.int32, signal.shape, 1)
    one = jnp.where(lane == 0, newer, pltpu.roll(signal, 1, 1))
    two = jnp.where(lane == 0, older, jnp.where(lane == 1, newer, pltpu.roll(signal, 2, 1)))
    return taps[0] * signal + taps[1] * one + taps[2] * two


def drive_kernel(keys_ref, values_ref, small_ref, packed_ref, drive_ref):
    for chan in range(8):
        rows = slice(16 * chan, 16 * chan + 16)
        col = lambda n: small_ref[rows, n : n + 1]
        key = feature(keys_ref[rows, :], [col(3), col(4), col(5)], col(12), col(13))
        value = feature(values_ref[rows, :], [col(6), col(7), col(8)], col(14), col(15))
        drive = key * value
        drive_ref[rows, :] = drive
        pack_rows(packed_ref, chan, drive, 0)


def gate_kernel(queries_ref, drive_ref, small_ref, gain_ref, direct_ref):
    for chan in range(8):
        rows = slice(16 * chan, 16 * chan + 16)
        col = lambda n: small_ref[rows, n : n + 1]
        query = feature(queries_ref[rows, :], [col(0), col(1), col(2)], col(10), col(11))
        gain_ref[rows, :] = query
        direct_ref[rows, :] = query * (col(9) * drive_ref[rows, :])


def finish_kernel(rows_ref, gain_ref, direct_ref, out_ref):
    for chan in range(8):
        rows = slice(16 * chan, 16 * chan + 16)
        for quarter in range(GROUP):
            for half in range(2):
                at = (2 * quarter + half) * LANES
                got = rows_ref[pl.ds(16 * quarter + 2 * chan + half, 16, stride=64), :]
                out_ref[rows, at : at + LANES] = gain_ref[rows, at : at + LANES] * got + direct_ref[rows, at : at + LANES]


def outer_kernel(me_ref, x_ref, high_ref, low_ref, *refs):
    outs, (xh_ref, xl_ref) = refs[:GROUP], refs[GROUP:]
    step = pl.program_id(0)

    @pl.when(step == 0)
    def _():
        for half in range(2):
            high, low = split(x_ref[pl.ds(half, ROWS, stride=2), :])
            xh_ref[:, half * LANES : (half + 1) * LANES] = high
            xl_ref[:, half * LANES : (half + 1) * LANES] = low

    xh = xh_ref[...]
    value = mm(high_ref[...], xh) + mm(high_ref[...], xl_ref[...]) + mm(low_ref[...], xh)
    for mask in range(GROUP):

        @pl.when(step == mask)
        def _(mask=mask):
            outs[mask][...] = value


def gather(me, pieces, held_ref):
    for mask in range(GROUP):
        held_ref[me ^ mask] = pieces[mask][...]


def butterfly(parts, sign):
    (ar, ai), (br, bi), (cr, ci), (dr, di) = parts
    er, ei, fr, fi = ar + cr, ai + ci, ar - cr, ai - ci
    gr, gi, hr, hi = br + dr, bi + di, sign * (br - dr), sign * (bi - di)
    return [(er + gr, ei + gi), (fr - hi, fi + hr), (er - gr, ei - gi), (fr + hi, fi - hr)]


def inner_product(real, imag, inner_ref):
    high, low = split(jnp.concatenate((real, imag), 0))
    result = mm(jnp.concatenate((high, low, high), 1), inner_ref[...])
    return result[:MINE, :QUARTER], result[:MINE, QUARTER:], result[MINE:, :QUARTER], result[MINE:, QUARTER:]


def spectrum(held_ref, turn_ref, step_ref, inner_ref):
    parts = []
    for s in range(GROUP):
        real, imag = held_ref[s, :MINE, :], held_ref[s, MINE:, :]
        cos, sin = turn_ref[0, 0, :, s * QUARTER : (s + 1) * QUARTER], turn_ref[0, 1, :, s * QUARTER : (s + 1) * QUARTER]
        parts.append((real * cos - imag * sin, real * sin + imag * cos))
    result = []
    for r, (real, imag) in enumerate(butterfly(parts, -1.0)):
        if r:
            cos, sin = step_ref[2 * r : 2 * r + 1, :], step_ref[2 * r + 1 : 2 * r + 2, :]
            real, imag = real * cos - imag * sin, real * sin + imag * cos
        rr, ri, ir, ii = inner_product(real, imag, inner_ref)
        result.append((rr - ii, ri + ir))
    return result


def filter_kernel(me_ref, p0, p1, p2, p3, turn_ref, step_ref, inner_ref, out_ref, held_ref):
    gather(me_ref[0], (p0, p1, p2, p3), held_ref)
    for r, (real, imag) in enumerate(spectrum(held_ref, turn_ref, step_ref, inner_ref)):
        out_ref[r, :MINE, :] = real
        out_ref[r, MINE:, :] = imag


def product_kernel(me_ref, p0, p1, p2, p3, filter_ref, turn_ref, step_ref, inner_ref, o0, o1, o2, o3, held_ref):
    me = me_ref[0]
    gather(me, (p0, p1, p2, p3), held_ref)
    parts = []
    for r, (real, imag) in enumerate(spectrum(held_ref, turn_ref, step_ref, inner_ref)):
        fr, fi = filter_ref[r, :MINE, :], filter_ref[r, MINE:, :]
        rr, ri, ir, ii = inner_product(real * fr - imag * fi, real * fi + imag * fr, inner_ref)
        real, imag = rr + ii, ir - ri
        if r:
            cos, sin = step_ref[2 * r : 2 * r + 1, :], step_ref[2 * r + 1 : 2 * r + 2, :]
            real, imag = real * cos + imag * sin, imag * cos - real * sin
        parts.append((real, imag))
    for s, (real, imag) in enumerate(butterfly(parts, 1.0)):
        cos, sin = turn_ref[0, 0, :, s * QUARTER : (s + 1) * QUARTER], turn_ref[0, 1, :, s * QUARTER : (s + 1) * QUARTER]
        held_ref[s, :MINE, :] = real * cos + imag * sin
        held_ref[s, MINE:, :] = imag * cos - real * sin
    for mask, out_ref in enumerate((o0, o1, o2, o3)):
        out_ref[...] = held_ref[me ^ mask]


def back_kernel(me_ref, p0, p1, p2, p3, high_ref, low_ref, out_ref, held_ref, zh_ref, zl_ref):
    @pl.when(pl.program_id(0) == 0)
    def _():
        gather(me_ref[0], (p0, p1, p2, p3), held_ref)
        for s in range(GROUP):
            high, low = split(held_ref[s])
            zh_ref[s * 2 * MINE : (s + 1) * 2 * MINE, :] = high
            zl_ref[s * 2 * MINE : (s + 1) * 2 * MINE, :] = low

    zh = zh_ref[...]
    value = mm(high_ref[...], zh) + mm(high_ref[...], zl_ref[...]) + mm(low_ref[...], zh)
    for half in range(2):
        out_ref[pl.ds(half, MINE, stride=2), :] = value[:, half * LANES : (half + 1) * LANES]


VMEM_LIMIT = 40 * 1024 * 1024


def call(kernel, out_shapes, args, grid=None, in_specs=None, out_specs=None, scratch=(), prefetch=0, flops=0):
    nbytes = sum(a.size * a.dtype.itemsize for a in args) + sum(int(np.prod(s.shape)) * 4 for s in out_shapes)
    single = len(out_shapes) == 1
    whole = lambda s: pl.BlockSpec(s.shape, lambda *_, n=len(s.shape): (0,) * n)
    in_specs = in_specs or [whole(a) for a in args[prefetch:]]
    out_specs = out_specs or [whole(s) for s in out_shapes]
    return pl.pallas_call(
        kernel,
        out_shape=out_shapes[0] if single else out_shapes,
        grid_spec=pltpu.PrefetchScalarGridSpec(
            num_scalar_prefetch=prefetch,
            grid=grid or (1,),
            in_specs=in_specs,
            out_specs=out_specs[0] if single else out_specs,
            scratch_shapes=list(scratch),
        ),
        compiler_params=pltpu.CompilerParams(vmem_limit_bytes=VMEM_LIMIT),
        cost_estimate=pl.CostEstimate(flops=flops, bytes_accessed=nbytes, transcendentals=0),
    )(*args)


def shape(*dims):
    return jax.ShapeDtypeStruct(dims, F32)


PIECE = (2 * MINE, QUARTER)


def exchange(pieces):
    moved = [pieces[0]]
    for mask in (2, 3, 1):
        size = lax.axis_size("seq")
        moved.append(lax.ppermute(pieces[mask], "seq", [(i, i ^ mask) for i in range(size)]))
    return [moved[0], moved[3], moved[1], moved[2]]


def outer(me, rows, forward):
    block = pl.BlockSpec((2 * MINE, ROWS), lambda i, me: (me[0] ^ i, 0))
    whole = pl.BlockSpec((2 * ROWS, LANES), lambda i, me: (0, 0))
    return call(
        outer_kernel,
        [shape(*PIECE)] * GROUP,
        (me, rows, *forward),
        grid=(GROUP,),
        in_specs=[whole, block, block],
        out_specs=[pl.BlockSpec(PIECE, lambda i, me: (0, 0))] * GROUP,
        scratch=[pltpu.VMEM((ROWS, QUARTER), BF)] * 2,
        prefetch=1,
        flops=3 * 2 * 2 * ROWS * ROWS * QUARTER,
    )


def middle(kernel, me, pieces, extra, turns, steps, inner3, outs, flops):
    whole = lambda s: pl.BlockSpec(s.shape, lambda i, me, n=len(s.shape): (0,) * n)
    turn = pl.BlockSpec((1, 2, MINE, COLS), lambda i, me: (me[0], 0, 0, 0))
    return call(
        kernel,
        outs,
        (me, *pieces, *extra, turns, steps, inner3),
        in_specs=[whole(a) for a in (*pieces, *extra)] + [turn, whole(steps), whole(inner3)],
        scratch=[pltpu.VMEM((GROUP, *PIECE), F32)],
        prefetch=1,
        flops=flops,
    )


def back(me, pieces, backward):
    block = pl.BlockSpec((MINE, 2 * ROWS), lambda i, me: (i, 0))
    piece = pl.BlockSpec(PIECE, lambda i, me: (0, 0))
    return call(
        back_kernel,
        [shape(2 * ROWS, LANES)],
        (me, *pieces, *backward),
        grid=(GROUP,),
        in_specs=[piece] * GROUP + [block, block],
        out_specs=[pl.BlockSpec((2 * MINE, LANES), lambda i, me: (i, 0))],
        scratch=[pltpu.VMEM((GROUP, *PIECE), F32)] + [pltpu.VMEM((2 * ROWS, QUARTER), BF)] * 2,
        prefetch=1,
        flops=3 * 2 * 2 * ROWS * ROWS * QUARTER,
    )


def swap(rows, axes, count):
    moved = lax.all_to_all(rows.reshape(count, -1, LANES), axes, 0, 0, tiled=True)
    return moved.reshape(2 * ROWS, LANES)


def local(queries, keys, values, short_taps, long_filter, skip_gain):
    everyone = ("seq", "chan")
    forward, backward, turns, steps, inner3 = jax.tree.map(jnp.asarray, tables())
    me = (lax.axis_index("seq") % GROUP).astype(jnp.int32).reshape(1)
    channels = queries.shape[0]

    filter_rows = call(pack_filter_kernel, [shape(2 * ROWS, LANES)], (long_filter,))
    filter_rows = swap(filter_rows, "seq", lax.axis_size("seq"))

    edges = jnp.stack((queries[:, -2], queries[:, -1], keys[:, -2], keys[:, -1], values[:, -2], values[:, -1]))
    size = lax.axis_size(everyone)
    before = lax.ppermute(edges, everyone, [(i, i + 1) for i in range(size - 1)])
    small = jnp.concatenate((short_taps.reshape(9, channels), skip_gain[None], before)).T
    packed, drive = call(drive_kernel, [shape(2 * ROWS, LANES), shape(channels, COLS)], (keys, values, small))
    drive_rows = swap(packed, everyone, size)

    middle_flops = 3 * 2 * 1024 * 256 * 512
    filter_pieces = exchange(outer(me, filter_rows, forward))
    spectra = middle(filter_kernel, me, filter_pieces, (), turns, steps, inner3, [shape(GROUP, *PIECE)], middle_flops)

    pieces = exchange(outer(me, drive_rows, forward))
    pieces = middle(
        product_kernel, me, pieces, (spectra,), turns, steps, inner3, [shape(*PIECE)] * GROUP, 2 * middle_flops
    )
    result = back(me, exchange(pieces), backward)
    gain, direct = call(gate_kernel, [shape(channels, COLS)] * 2, (queries, drive, small))
    returned = swap(result, everyone, size)
    return call(finish_kernel, [shape(channels, COLS)], (returned, gain, direct))


def solution(mesh):
    spread = P(None, ("seq", "chan"))
    in_specs = (spread, spread, spread, P(), P("chan", "seq"), P())
    return jax.shard_map(local, mesh=mesh, in_specs=in_specs, out_specs=spread, check_vma=False)
```

```python
import functools

import jax
import jax.numpy as jnp
import numpy as np
from jax import lax
from jax.experimental import pallas as pl
from jax.experimental.pallas import tpu as pltpu
from jax.sharding import PartitionSpec as P


BF = jnp.bfloat16
F32 = jnp.float32
GROUP = 4
ROWS = 512
COLS = 1024
Q = 256
LANES = 128
TILES = 8
CHUNK = 16
TOTAL = ROWS * COLS
ROOT = float(np.sqrt(0.5))


def halves(values):
    high = np.asarray(values, np.float32).astype(jnp.bfloat16)
    low = (np.asarray(values, np.float64) - high.astype(np.float64)).astype(np.float32).astype(jnp.bfloat16)
    return high, low


@functools.lru_cache(maxsize=None)
def tables():
    i = np.arange(LANES, dtype=np.float64)
    grid = 2.0 * np.pi * np.outer(i, i) / LANES
    cos, sin = np.cos(grid), np.sin(grid)
    ahead = np.block([[cos, -sin], [sin, cos]])
    matrices = np.stack((*halves(ahead), *halves(ahead.T)))
    steps = np.zeros((2, 2 * TILES, LANES))
    for r in range(TILES):
        angle = 2.0 * np.pi * r * i / COLS
        for chip in range(2):
            sign = -1.0 if chip and r % 2 else 1.0
            steps[chip, 2 * r], steps[chip, 2 * r + 1] = sign * np.cos(angle), -sign * np.sin(angle)
    turns = np.zeros((2, 2, Q, LANES))
    columns = np.zeros((GROUP, Q, LANES))
    mixes = np.zeros((2, LANES, LANES))
    for member in range(GROUP):
        chip, core = divmod(member, 2)
        k1 = np.concatenate((4.0 * i + core, 4.0 * i + 2.0 + core)) + 0.25
        angle = 2.0 * np.pi * np.outer(k1, i) / TOTAL
        turns[core, 0], turns[core, 1] = np.cos(angle), -np.sin(angle)
        for s in range(TILES):
            angle = 2.0 * np.pi * s * LANES * k1 / TOTAL
            columns[member, :, 2 * s], columns[member, :, 2 * s + 1] = np.cos(angle), -np.sin(angle)
        columns[member, :, 16:24] = columns[member, :, 8 * chip : 8 * chip + 8]
        for a in range(4):
            for q in range(2):
                angle = 2.0 * np.pi * (a * LANES + i) * (2.0 * q + core + 0.25) / ROWS
                at = 4 * a + 2 * q
                mixes[core, :, at], mixes[core, :, at + 1] = np.cos(angle), -np.sin(angle)
                mixes[core, :, 16 + at], mixes[core, :, 17 + at] = np.cos(angle) / TOTAL, -np.sin(angle) / TOTAL
    pages = []
    for member in range(GROUP):
        chip, core = divmod(member, 2)
        pages.append(
            np.concatenate((columns[member], turns[core, 0], turns[core, 1], mixes[core], mixes[1 - core], steps[chip], steps[0]))
        )
    return matrices, np.stack(pages).astype(np.float32)


def split(x):
    high = x.astype(BF)
    return high, (x - high.astype(F32)).astype(BF)


def mm(a, b):
    return jnp.dot(a, b, preferred_element_type=F32)


def pack_filter_kernel(filter_rows, out_ref, held_ref, sem_ref):
    width = filter_rows.shape[1] // 4
    pieces = [filter_rows.at[:, pl.ds(n * width, width)] for n in range(4)]
    loads = Loads(sem_ref, [(piece, held_ref.at[n]) for n, piece in enumerate(pieces)])
    for n in range(4):
        loads.wait(n)
        for tile in range(width // LANES):
            out_ref[pl.ds(n * (width // LANES) + tile, 16, stride=64), :] = held_ref[n, :, tile * LANES : (tile + 1) * LANES]


def feature(signal, taps, older, newer):
    lane = lax.broadcasted_iota(jnp.int32, signal.shape, 1)
    one = jnp.where(lane == 0, newer, pltpu.roll(signal, 1, 1))
    two = jnp.where(lane == 0, older, jnp.where(lane == 1, newer, pltpu.roll(signal, 2, 1)))
    return taps[0] * signal + taps[1] * one + taps[2] * two


def drive_kernel(keys_ref, values_ref, small_ref, packed_ref, drive_ref, token_ref):
    token_ref[...] = small_ref[:8, :16]
    for chan in range(8):
        rows = slice(16 * chan, 16 * chan + 16)
        col = lambda n: small_ref[rows, n : n + 1]
        key = feature(keys_ref[rows, :], [col(3), col(4), col(5)], col(12), col(13))
        value = feature(values_ref[rows, :], [col(6), col(7), col(8)], col(14), col(15))
        drive = key * value
        drive_ref[rows, :] = drive
        for member in range(GROUP):
            for half in range(2):
                at = (2 * member + half) * LANES
                packed_ref[pl.ds(16 * member + 2 * chan + half, 16, stride=64), :] = drive[:, at : at + LANES]


def gate_kernel(queries_ref, drive_ref, small_ref, gain_ref, direct_ref):
    for chan in range(8):
        rows = slice(16 * chan, 16 * chan + 16)
        col = lambda n: small_ref[rows, n : n + 1]
        query = feature(queries_ref[rows, :], [col(0), col(1), col(2)], col(10), col(11))
        gain_ref[rows, :] = query
        direct_ref[rows, :] = query * (col(9) * drive_ref[rows, :])


def finish_kernel(rows_ref, gain_ref, direct_ref, out_ref):
    for chan in range(8):
        rows = slice(16 * chan, 16 * chan + 16)
        for core in range(2):
            for tile in range(4):
                at = (4 * core + tile) * LANES
                first = rows_ref[pl.ds(32 * core + 4 * chan + tile, 16, stride=128), :]
                second = rows_ref[pl.ds(32 * (2 + core) + 4 * chan + tile, 16, stride=128), :]
                out_ref[rows, at : at + LANES] = (
                    gain_ref[rows, at : at + LANES] * (first + second) + direct_ref[rows, at : at + LANES]
                )


def times(a, b, conjugate=False):
    (ar, ai), (br, bi) = a, b
    if conjugate:
        return ar * br + ai * bi, ai * br - ar * bi
    return ar * br - ai * bi, ar * bi + ai * br


def mixed(weights, values):
    (w0, w1, w2, w3), (v0, v1, v2, v3) = weights, values
    return (w0 * v0 + w1 * v1) + (w2 * v2 + w3 * v3)


def plus(a, b):
    return a[0] + b[0], a[1] + b[1]


def minus(a, b):
    return a[0] - b[0], a[1] - b[1]


def turned(a, sign):
    return (-a[1], a[0]) if sign > 0 else (a[1], -a[0])


def eighth(a, power, sign):
    if power >= 2:
        a = turned(a, sign)
    if power % 2:
        real, imag = a
        a = ((real - sign * imag) * ROOT, (imag + sign * real) * ROOT)
    return a


def four(parts, sign):
    e, f = plus(parts[0], parts[2]), minus(parts[0], parts[2])
    g, h = plus(parts[1], parts[3]), turned(minus(parts[1], parts[3]), sign)
    return [plus(e, g), plus(f, h), minus(e, g), minus(f, h)]


TURN, MIX, STEP, PAGE = Q, 3 * Q, 4 * Q, 4 * Q + 4 * TILES


def column(page_ref, rows, n):
    return page_ref[rows, n : n + 1], page_ref[rows, n + 1 : n + 2]


def turn(page_ref, rows):
    return tuple(page_ref[TURN + part * Q + rows.start : TURN + part * Q + rows.stop, :] for part in range(2))


def mixes(page_ref, other, rows, first):
    at = MIX + other * LANES
    return [page_ref[at + rows.start : at + rows.stop, n : n + 1] for n in range(first, first + 16)]


def step(page_ref, plain, r):
    at = STEP + plain * 2 * TILES + 2 * r
    return page_ref[at : at + 1, :], page_ref[at + 1 : at + 2, :]


class Loads:
    def __init__(self, sem_ref, pairs):
        self.copies = [pltpu.make_async_copy(src, dst, sem_ref.at[n]) for n, (src, dst) in enumerate(pairs)]
        for copy in self.copies:
            copy.start()

    def wait(self, *which):
        for n in which:
            self.copies[n].wait()


def matrix(ref, transposed, axis):
    high, low = ref[2 * transposed], ref[2 * transposed + 1]
    return jnp.concatenate((high, high, low), axis)


def left_product(matrix_ref, transposed, high, low):
    return mm(matrix(matrix_ref, transposed, 1), jnp.concatenate((high, low, high), 0))


def right_product(matrix_ref, transposed, high, low):
    return mm(jnp.concatenate((high, low, high), 1), matrix(matrix_ref, transposed, 0))


def outer_transform(x_ref, count, other, page_ref, matrix_ref, f_ref, high_ref, low_ref):
    for chunk in range(LANES // CHUNK):
        rows = slice(chunk * CHUNK, (chunk + 1) * CHUNK)
        mix = mixes(page_ref, other, rows, 0)
        for s in range(count):
            x = [x_ref[s, a * LANES + rows.start : a * LANES + rows.stop, :] for a in range(4)]
            for q in range(2):
                for part in range(2):
                    u = mixed([mix[4 * a + 2 * q + part] for a in range(4)], x)
                    at = slice(part * LANES + rows.start, part * LANES + rows.stop), slice(q * LANES, (q + 1) * LANES)
                    high_ref[s, *at], low_ref[s, *at] = split(u)
    for s in range(count):
        result = left_product(matrix_ref, 1, high_ref[s], low_ref[s])
        for part in range(2):
            for q in range(2):
                f_ref[s, part, q * LANES : (q + 1) * LANES, :] = result[
                    part * LANES : (part + 1) * LANES, q * LANES : (q + 1) * LANES
                ]


def inner_transform(f_ref, count, plain, first, page_ref, high_ref, low_ref):
    for chunk in range(Q // CHUNK):
        rows = slice(chunk * CHUNK, (chunk + 1) * CHUNK)
        angle = turn(page_ref, rows)
        parts = [
            times(times((f_ref[s, 0, rows, :], f_ref[s, 1, rows, :]), angle), column(page_ref, rows, first + 2 * s))
            for s in range(count)
        ]
        if count == TILES:
            even = [plus(parts[s], parts[s + 4]) for s in range(4)]
            odd = [minus(parts[s], parts[s + 4]) for s in range(4)]
        else:
            even = odd = parts
        even, odd = four(even, -1), four([eighth(odd[s], s, -1) for s in range(4)], -1)
        for r in range(TILES):
            value = (odd if r % 2 else even)[r // 2]
            if r:
                value = times(value, step(page_ref, plain, r))
            for part in range(2):
                at = rows, slice(part * LANES, (part + 1) * LANES)
                high_ref[r, *at], low_ref[r, *at] = split(value[part])


def filter_kernel(
    me_ref, pages, matrices, p0, p1, p2, p3, out_ref, token_ref, page_ref, matrix_ref, sem_ref, held_ref, x_ref, f_ref, high_ref, low_ref
):
    me = me_ref[0]
    pieces = [(piece, held_ref.at[mask]) for mask, piece in enumerate((p0, p1, p2, p3))]
    loads = Loads(sem_ref, [(pages.at[me], page_ref), (matrices, matrix_ref), *pieces])
    for mask in range(GROUP):
        loads.wait(2 + mask)
        at = (me ^ mask) * 8
        for a in range(16):
            for tile in range(TILES):
                rows = pl.ds(pl.multiple_of(a * 32 + at, 8), 8)
                x_ref[tile, rows, :] = held_ref[mask, pl.ds(a * 64 + tile, 8, stride=8), :]
    loads.wait(0, 1)
    token_ref[...] = page_ref[:8, :]
    outer_transform(x_ref, TILES, 0, page_ref, matrix_ref, f_ref, high_ref, low_ref)
    inner_transform(f_ref, TILES, 1, 0, page_ref, high_ref, low_ref)
    for r in range(TILES):
        out_ref[r] = right_product(matrix_ref, 0, high_ref[r], low_ref[r])


def drive_outer_kernel(
    me_ref, pages, matrices, own_ref, _, mine_ref, other_ref, page_ref, matrix_ref, sem_ref, x_ref, high_ref, low_ref
):
    loads = Loads(sem_ref, [(pages.at[me_ref[0]], page_ref), (matrices, matrix_ref)])
    for half in range(2):
        x_ref[half] = own_ref[pl.ds(half, ROWS, stride=2), :]
    loads.wait(0, 1)
    outer_transform(x_ref, 2, 1, page_ref, matrix_ref, other_ref, high_ref, low_ref)
    outer_transform(x_ref, 2, 0, page_ref, matrix_ref, mine_ref, high_ref, low_ref)


def product_kernel(
    me_ref,
    pages,
    matrices,
    own,
    peer,
    spectrum,
    mine_ref,
    other_ref,
    page_ref,
    matrix_ref,
    sem_ref,
    f_ref,
    filter_ref,
    d_ref,
    high_ref,
    low_ref,
):
    me = me_ref[0]
    core = me & 1
    pieces = [(own, f_ref.at[pl.ds(2 * core, 2)]), (peer, f_ref.at[pl.ds(2 * (1 - core), 2)])]
    loads = Loads(sem_ref, [(pages.at[me], page_ref), (matrices, matrix_ref), *pieces, (spectrum, filter_ref)])
    loads.wait(0, 2, 3)
    inner_transform(f_ref, 4, 0, 16, page_ref, high_ref, low_ref)
    loads.wait(1, 4)
    for r in range(TILES):
        x, h = right_product(matrix_ref, 0, high_ref[r], low_ref[r]), filter_ref[r]
        value = times((x[:, :LANES], x[:, LANES:]), (h[:, :LANES], h[:, LANES:]))
        d_ref[r] = right_product(matrix_ref, 1, *split(jnp.concatenate(value, 1)))
    for chunk in range(Q // CHUNK):
        rows = slice(chunk * CHUNK, (chunk + 1) * CHUNK)
        q, kappa = divmod(chunk * CHUNK, LANES)
        angle = turn(page_ref, rows)
        parts = []
        for r in range(TILES):
            value = d_ref[r, rows, :LANES], d_ref[r, rows, LANES:]
            if r:
                value = times(value, step(page_ref, 1, r), True)
            parts.append(value)
        even, odd = four(parts[0::2], 1), four(parts[1::2], 1)
        odd = [eighth(odd[s], s, 1) for s in range(4)]
        for s in range(TILES):
            value = (minus if s >= 4 else plus)(even[s % 4], odd[s % 4])
            value = times(times(value, angle, True), column(page_ref, rows, 2 * s), True)
            for part in range(2):
                at = slice(part * LANES + kappa, part * LANES + kappa + CHUNK), slice(q * LANES, (q + 1) * LANES)
                high_ref[s, *at], low_ref[s, *at] = split(value[part])
    for s in range(TILES):
        d_ref[s] = left_product(matrix_ref, 0, high_ref[s], low_ref[s])
    for chunk in range(LANES // CHUNK):
        rows = slice(chunk * CHUNK, (chunk + 1) * CHUNK)
        mix = mixes(page_ref, 0, rows, 16)
        for owner, out_ref in ((core, mine_ref), (1 - core, other_ref)):
            for t in range(4):
                s = 4 * owner + t
                v = [
                    d_ref[s, part * LANES + rows.start : part * LANES + rows.stop, q * LANES : (q + 1) * LANES]
                    for q in range(2)
                    for part in range(2)
                ]
                for a in range(4):
                    value = mixed(mix[4 * a : 4 * a + 4], v)
                    out_ref[pl.ds((a * LANES + rows.start) * 4 + t, CHUNK, stride=4), :] = value


VMEM_LIMIT = 32 * 1024 * 1024
VMEM_ALL = 60 * 1024 * 1024
FILTER_FLOPS = 3 * 2 * 256 * 256 * 256 * 16


def whole(s):
    return pl.BlockSpec(s.shape, lambda *_, n=len(s.shape): (0,) * n)


def call(kernel, out_shapes, args, in_specs=None, scratch=(), prefetch=0, flops=0, limit=VMEM_LIMIT):
    nbytes = sum(a.size * a.dtype.itemsize for a in args) + sum(int(np.prod(s.shape)) * 4 for s in out_shapes)
    single = len(out_shapes) == 1
    out_specs = [whole(s) for s in out_shapes]
    return pl.pallas_call(
        kernel,
        out_shape=out_shapes[0] if single else out_shapes,
        grid_spec=pltpu.PrefetchScalarGridSpec(
            num_scalar_prefetch=prefetch,
            grid=(1,),
            in_specs=in_specs or [whole(a) for a in args[prefetch:]],
            out_specs=out_specs[0] if single else out_specs,
            scratch_shapes=list(scratch),
        ),
        compiler_params=pltpu.CompilerParams(vmem_limit_bytes=limit),
        cost_estimate=pl.CostEstimate(flops=flops, bytes_accessed=nbytes, transcendentals=0),
    )(*args)


def shape(*dims):
    return jax.ShapeDtypeStruct(dims, F32)


HBM = pl.BlockSpec(memory_space=pltpu.HBM)


def transform(kernel, me, arrays, specs, outs, scratch, flops):
    matrices, pages = map(jnp.asarray, tables())
    fixed = [
        pltpu.VMEM((PAGE, LANES), F32),
        pltpu.VMEM(matrices.shape, BF),
        pltpu.SemaphoreType.DMA((2 + specs.count(HBM),)),
    ]
    count = 2 if kernel is drive_outer_kernel else TILES
    scratch = fixed + [pltpu.VMEM(s, F32) for s in scratch] + [pltpu.VMEM((count, Q, Q), BF)] * 2
    limit = VMEM_ALL if kernel is filter_kernel else VMEM_LIMIT
    return call(kernel, outs, (me, pages, matrices, *arrays), [HBM, HBM, *specs], scratch, 1, flops, limit)


def tie_kernel(rows_ref, _, out_ref):
    pass


def after(rows, other):
    return pl.pallas_call(
        tie_kernel,
        out_shape=shape(*rows.shape),
        grid=(1,),
        in_specs=[pl.BlockSpec(memory_space=pl.ANY), whole(other)],
        out_specs=pl.BlockSpec(memory_space=pl.ANY),
        input_output_aliases={0: 0},
        compiler_params=pltpu.CompilerParams(vmem_limit_bytes=VMEM_LIMIT),
    )(rows, other)


def across(rows, mask):
    size = lax.axis_size("seq")
    return lax.ppermute(rows, "seq", [(i, i ^ mask) for i in range(size)])


def local(queries, keys, values, short_taps, long_filter, skip_gain):
    everyone = ("seq", "chan")
    size = lax.axis_size(everyone)
    seq_size = lax.axis_size("seq")
    me = (lax.axis_index("seq") % GROUP).astype(jnp.int32).reshape(1)
    channels = queries.shape[0]

    held = [pltpu.VMEM((4, 16, 2 * COLS), F32), pltpu.SemaphoreType.DMA((4,))]
    filter_rows = call(pack_filter_kernel, [shape(2 * ROWS, LANES)], (long_filter,), [HBM], held, limit=VMEM_ALL)
    alike = [list(range(member, seq_size, GROUP)) for member in range(GROUP)]
    filter_rows = lax.all_to_all(
        filter_rows.reshape(16, 64, LANES), "seq", 0, 0, tiled=True, axis_index_groups=alike
    ).reshape(2 * ROWS, LANES)

    edges = jnp.stack((queries[:, -2], queries[:, -1], keys[:, -2], keys[:, -1], values[:, -2], values[:, -1]))
    before = lax.ppermute(edges, everyone, [(i, i + 1) for i in range(size - 1)])
    small = jnp.concatenate((short_taps.reshape(9, channels), skip_gain[None], before)).T
    outs = [shape(2 * ROWS, LANES), shape(channels, COLS), shape(8, 16)]
    packed, drive, token = call(drive_kernel, outs, (keys, values, small))
    filter_rows = after(filter_rows, token)
    filter_far = across(filter_rows, 2)
    own = lax.all_to_all(packed.reshape(size, -1, LANES), everyone, 0, 0, tiled=True).reshape(2 * ROWS, LANES)

    flops = 3 * 2 * 256 * 256 * 256 * 8
    pieces = (filter_rows, across(filter_rows, 1), filter_far, across(filter_far, 1))
    filter_spectrum, token = transform(
        filter_kernel,
        me,
        pieces,
        [HBM] * GROUP,
        [shape(TILES, Q, Q), shape(8, LANES)],
        [(GROUP, 2 * ROWS, LANES), (TILES, ROWS, LANES), (TILES, 2, Q, LANES)],
        FILTER_FLOPS,
    )
    mine, other = transform(
        drive_outer_kernel,
        me,
        (own, token),
        [whole(own), whole(token)],
        [shape(2, 2, Q, LANES)] * 2,
        [(2, ROWS, LANES)],
        flops,
    )
    mine, other = transform(
        product_kernel,
        me,
        (mine, across(other, 1), filter_spectrum),
        [HBM] * 3,
        [shape(4 * ROWS, LANES)] * 2,
        [(4, 2, Q, LANES), (TILES, Q, Q), (TILES, Q, Q)],
        3 * flops,
    )
    result = mine + across(other, 1)
    gain, direct = call(gate_kernel, [shape(channels, COLS)] * 2, (queries, drive, small))
    returned = lax.all_to_all(result.reshape(size, -1, LANES), everyone, 0, 0, tiled=True).reshape(4 * ROWS, LANES)
    return call(finish_kernel, [shape(channels, COLS)], (returned, gain, direct))


def solution(mesh):
    spread = P(None, ("seq", "chan"))
    in_specs = (spread, spread, spread, P(), P("chan", "seq"), P())
    return jax.shard_map(local, mesh=mesh, in_specs=in_specs, out_specs=spread, check_vma=False)
```

```python
import functools

import jax
import jax.numpy as jnp
import numpy as np
from jax import lax
from jax.experimental import pallas as pl
from jax.experimental.pallas import tpu as pltpu
from jax.sharding import PartitionSpec as P


BF = jnp.bfloat16
F32 = jnp.float32
GROUP = 4
ROWS = 512
COLS = 1024
Q = 256
LANES = 128
TILES = 8
CHUNK = 16
TOTAL = ROWS * COLS
ROOT = float(np.sqrt(0.5))


def halves(values):
    high = np.asarray(values, np.float32).astype(jnp.bfloat16)
    low = (np.asarray(values, np.float64) - high.astype(np.float64)).astype(np.float32).astype(jnp.bfloat16)
    return high, low


@functools.lru_cache(maxsize=None)
def tables():
    i = np.arange(LANES, dtype=np.float64)
    grid = 2.0 * np.pi * np.outer(i, i) / LANES
    cos, sin = np.cos(grid), np.sin(grid)
    ahead = np.block([[cos, -sin], [sin, cos]])
    matrices = np.stack((*halves(ahead), *halves(ahead.T)))
    steps = np.zeros((2, 2 * TILES, LANES))
    for r in range(TILES):
        angle = 2.0 * np.pi * r * i / COLS
        for chip in range(2):
            sign = -1.0 if chip and r % 2 else 1.0
            steps[chip, 2 * r], steps[chip, 2 * r + 1] = sign * np.cos(angle), -sign * np.sin(angle)
    turns = np.zeros((2, 2, Q, LANES))
    columns = np.zeros((GROUP, Q, LANES))
    mixes = np.zeros((2, LANES, LANES))
    for member in range(GROUP):
        chip, core = divmod(member, 2)
        k1 = np.concatenate((4.0 * i + core, 4.0 * i + 2.0 + core)) + 0.25
        angle = 2.0 * np.pi * np.outer(k1, i) / TOTAL
        turns[core, 0], turns[core, 1] = np.cos(angle), -np.sin(angle)
        for s in range(TILES):
            angle = 2.0 * np.pi * s * LANES * k1 / TOTAL
            columns[member, :, 2 * s], columns[member, :, 2 * s + 1] = np.cos(angle), -np.sin(angle)
        columns[member, :, 16:24] = columns[member, :, 8 * chip : 8 * chip + 8]
        for a in range(4):
            for q in range(2):
                angle = 2.0 * np.pi * (a * LANES + i) * (2.0 * q + core + 0.25) / ROWS
                at = 4 * a + 2 * q
                mixes[core, :, at], mixes[core, :, at + 1] = np.cos(angle), -np.sin(angle)
                mixes[core, :, 16 + at], mixes[core, :, 17 + at] = np.cos(angle) / TOTAL, -np.sin(angle) / TOTAL
    pages = []
    for member in range(GROUP):
        chip, core = divmod(member, 2)
        pages.append(
            np.concatenate((columns[member], turns[core, 0], turns[core, 1], mixes[core], mixes[1 - core], steps[chip], steps[0]))
        )
    return matrices, np.stack(pages).astype(np.float32)


def split(x):
    high = x.astype(BF)
    return high, (x - high.astype(F32)).astype(BF)


def mm(a, b):
    return jnp.dot(a, b, preferred_element_type=F32)


def pack_filter_kernel(filter_rows, out_ref, held_ref, sem_ref):
    width = filter_rows.shape[1] // 4
    pieces = [filter_rows.at[:, pl.ds(n * width, width)] for n in range(4)]
    loads = Loads(sem_ref, [(piece, held_ref.at[n]) for n, piece in enumerate(pieces)])
    for n in range(4):
        loads.wait(n)
        for tile in range(width // LANES):
            out_ref[pl.ds(n * (width // LANES) + tile, 16, stride=64), :] = held_ref[n, :, tile * LANES : (tile + 1) * LANES]


def feature(signal, taps, older, newer):
    lane = lax.broadcasted_iota(jnp.int32, signal.shape, 1)
    one = jnp.where(lane == 0, newer, pltpu.roll(signal, 1, 1))
    two = jnp.where(lane == 0, older, jnp.where(lane == 1, newer, pltpu.roll(signal, 2, 1)))
    return taps[0] * signal + taps[1] * one + taps[2] * two


def drive_kernel(keys_ref, values_ref, small_ref, packed_ref, drive_ref, token_ref):
    token_ref[...] = small_ref[:8, :16]
    for chan in range(8):
        rows = slice(16 * chan, 16 * chan + 16)
        col = lambda n: small_ref[rows, n : n + 1]
        key = feature(keys_ref[rows, :], [col(3), col(4), col(5)], col(12), col(13))
        value = feature(values_ref[rows, :], [col(6), col(7), col(8)], col(14), col(15))
        drive = key * value
        drive_ref[rows, :] = drive
        for member in range(GROUP):
            for half in range(2):
                at = (2 * member + half) * LANES
                packed_ref[pl.ds(16 * member + 2 * chan + half, 16, stride=64), :] = drive[:, at : at + LANES]


def gate_kernel(queries_ref, drive_ref, small_ref, gain_ref, direct_ref):
    for chan in range(8):
        rows = slice(16 * chan, 16 * chan + 16)
        col = lambda n: small_ref[rows, n : n + 1]
        query = feature(queries_ref[rows, :], [col(0), col(1), col(2)], col(10), col(11))
        gain_ref[rows, :] = query
        direct_ref[rows, :] = query * (col(9) * drive_ref[rows, :])


def finish_kernel(rows_ref, gain_ref, direct_ref, out_ref):
    for chan in range(8):
        rows = slice(16 * chan, 16 * chan + 16)
        for core in range(2):
            for tile in range(4):
                at = (4 * core + tile) * LANES
                first = rows_ref[pl.ds(32 * core + 4 * chan + tile, 16, stride=128), :]
                second = rows_ref[pl.ds(32 * (2 + core) + 4 * chan + tile, 16, stride=128), :]
                out_ref[rows, at : at + LANES] = (
                    gain_ref[rows, at : at + LANES] * (first + second) + direct_ref[rows, at : at + LANES]
                )


def times(a, b, conjugate=False):
    (ar, ai), (br, bi) = a, b
    if conjugate:
        return ar * br + ai * bi, ai * br - ar * bi
    return ar * br - ai * bi, ar * bi + ai * br


def mixed(weights, values):
    (w0, w1, w2, w3), (v0, v1, v2, v3) = weights, values
    return (w0 * v0 + w1 * v1) + (w2 * v2 + w3 * v3)


def plus(a, b):
    return a[0] + b[0], a[1] + b[1]


def minus(a, b):
    return a[0] - b[0], a[1] - b[1]


def turned(a, sign):
    return (-a[1], a[0]) if sign > 0 else (a[1], -a[0])


def eighth(a, power, sign):
    if power >= 2:
        a = turned(a, sign)
    if power % 2:
        real, imag = a
        a = ((real - sign * imag) * ROOT, (imag + sign * real) * ROOT)
    return a


def four(parts, sign):
    e, f = plus(parts[0], parts[2]), minus(parts[0], parts[2])
    g, h = plus(parts[1], parts[3]), turned(minus(parts[1], parts[3]), sign)
    return [plus(e, g), plus(f, h), minus(e, g), minus(f, h)]


TURN, MIX, STEP, PAGE = Q, 3 * Q, 4 * Q, 4 * Q + 4 * TILES


def column(page_ref, rows, n):
    return page_ref[rows, n : n + 1], page_ref[rows, n + 1 : n + 2]


def turn(page_ref, rows):
    return tuple(page_ref[TURN + part * Q + rows.start : TURN + part * Q + rows.stop, :] for part in range(2))


def mixes(page_ref, other, rows, first, base=MIX):
    at = base + other * LANES
    return [page_ref[at + rows.start : at + rows.stop, n : n + 1] for n in range(first, first + 16)]


def step(page_ref, plain, r):
    at = STEP + plain * 2 * TILES + 2 * r
    return page_ref[at : at + 1, :], page_ref[at + 1 : at + 2, :]


class Loads:
    def __init__(self, sem_ref, pairs):
        self.copies = [pltpu.make_async_copy(src, dst, sem_ref.at[n]) for n, (src, dst) in enumerate(pairs)]
        for copy in self.copies:
            copy.start()

    def wait(self, *which):
        for n in which:
            self.copies[n].wait()


def matrix(ref, transposed, axis):
    high, low = ref[2 * transposed], ref[2 * transposed + 1]
    return jnp.concatenate((high, high, low), axis)


def left_product(matrix_ref, transposed, high, low):
    return mm(matrix(matrix_ref, transposed, 1), jnp.concatenate((high, low, high), 0))


def right_product(matrix_ref, transposed, high, low):
    return mm(jnp.concatenate((high, low, high), 1), matrix(matrix_ref, transposed, 0))


def outer_transform(x_ref, count, other, page_ref, base, matrix_ref, transposed, f_ref, high_ref, low_ref):
    for chunk in range(LANES // CHUNK):
        rows = slice(chunk * CHUNK, (chunk + 1) * CHUNK)
        mix = mixes(page_ref, other, rows, 0, base)
        for s in range(count):
            x = [x_ref[s, a * LANES + rows.start : a * LANES + rows.stop, :] for a in range(4)]
            for q in range(2):
                for part in range(2):
                    u = mixed([mix[4 * a + 2 * q + part] for a in range(4)], x)
                    at = slice(part * LANES + rows.start, part * LANES + rows.stop), slice(q * LANES, (q + 1) * LANES)
                    high_ref[s, *at], low_ref[s, *at] = split(u)
    for s in range(count):
        result = left_product(matrix_ref, transposed, high_ref[s], low_ref[s])
        for part in range(2):
            for q in range(2):
                f_ref[s, part, q * LANES : (q + 1) * LANES, :] = result[
                    part * LANES : (part + 1) * LANES, q * LANES : (q + 1) * LANES
                ]


def inner_transform(f_ref, count, plain, first, page_ref, high_ref, low_ref):
    for chunk in range(Q // CHUNK):
        rows = slice(chunk * CHUNK, (chunk + 1) * CHUNK)
        angle = turn(page_ref, rows)
        parts = [
            times(times((f_ref[s, 0, rows, :], f_ref[s, 1, rows, :]), angle), column(page_ref, rows, first + 2 * s))
            for s in range(count)
        ]
        if count == TILES:
            even = [plus(parts[s], parts[s + 4]) for s in range(4)]
            odd = [minus(parts[s], parts[s + 4]) for s in range(4)]
        else:
            even = odd = parts
        even, odd = four(even, -1), four([eighth(odd[s], s, -1) for s in range(4)], -1)
        for r in range(TILES):
            value = (odd if r % 2 else even)[r // 2]
            if r:
                value = times(value, step(page_ref, plain, r))
            for part in range(2):
                at = rows, slice(part * LANES, (part + 1) * LANES)
                high_ref[r, *at], low_ref[r, *at] = split(value[part])


def filter_kernel(
    me_ref, pages, matrices, p0, p1, p2, p3, out_ref, page_ref, matrix_ref, sem_ref, held_ref, x_ref, f_ref, high_ref, low_ref
):
    me = me_ref[0]
    pieces = [(piece, held_ref.at[mask]) for mask, piece in enumerate((p0, p1, p2, p3))]
    loads = Loads(sem_ref, [(pages.at[me], page_ref), (matrices, matrix_ref), *pieces])
    for mask in range(GROUP):
        loads.wait(2 + mask)
        at = (me ^ mask) * 8
        for a in range(16):
            for tile in range(TILES):
                rows = pl.ds(pl.multiple_of(a * 32 + at, 8), 8)
                x_ref[tile, rows, :] = held_ref[mask, pl.ds(a * 64 + tile, 8, stride=8), :]
    loads.wait(0, 1)
    outer_transform(x_ref, TILES, 0, page_ref, MIX, matrix_ref, 1, f_ref, high_ref, low_ref)
    inner_transform(f_ref, TILES, 1, 0, page_ref, high_ref, low_ref)
    for r in range(TILES):
        out_ref[r] = right_product(matrix_ref, 0, high_ref[r], low_ref[r])


def drive_outer_kernel(
    me_ref,
    pages,
    matrices,
    own_ref,
    spectrum,
    mine_ref,
    other_ref,
    page_ref,
    matrix_ref,
    filter_ref,
    mix_ref,
    ahead_ref,
    sem_ref,
    x_ref,
    high_ref,
    low_ref,
):
    page = pages.at[me_ref[0]]
    first = [(page.at[pl.ds(MIX, 2 * LANES)], mix_ref), (matrices.at[pl.ds(2, 2)], ahead_ref)]
    loads = Loads(sem_ref, [*first, (page, page_ref), (matrices, matrix_ref), (spectrum, filter_ref)])
    for half in range(2):
        x_ref[half] = own_ref[pl.ds(half, ROWS, stride=2), :]
    loads.wait(0, 1)
    outer_transform(x_ref, 2, 1, mix_ref, 0, ahead_ref, 0, other_ref, high_ref, low_ref)
    outer_transform(x_ref, 2, 0, mix_ref, 0, ahead_ref, 0, mine_ref, high_ref, low_ref)
    loads.wait(2, 3, 4)


def product_kernel(
    me_ref, own_ref, peer_ref, page_ref, matrix_ref, filter_ref, mine_ref, other_ref, f_ref, d_ref, high_ref, low_ref
):
    core = me_ref[0] & 1
    for which, piece_ref in ((core, own_ref), (1 - core, peer_ref)):
        for half in range(2):
            f_ref[2 * which + half] = piece_ref[half]
    inner_transform(f_ref, 4, 0, 16, page_ref, high_ref, low_ref)
    for r in range(TILES):
        x, h = right_product(matrix_ref, 0, high_ref[r], low_ref[r]), filter_ref[r]
        value = times((x[:, :LANES], x[:, LANES:]), (h[:, :LANES], h[:, LANES:]))
        d_ref[r] = right_product(matrix_ref, 1, *split(jnp.concatenate(value, 1)))
    for chunk in range(Q // CHUNK):
        rows = slice(chunk * CHUNK, (chunk + 1) * CHUNK)
        q, kappa = divmod(chunk * CHUNK, LANES)
        angle = turn(page_ref, rows)
        parts = []
        for r in range(TILES):
            value = d_ref[r, rows, :LANES], d_ref[r, rows, LANES:]
            if r:
                value = times(value, step(page_ref, 1, r), True)
            parts.append(value)
        even, odd = four(parts[0::2], 1), four(parts[1::2], 1)
        odd = [eighth(odd[s], s, 1) for s in range(4)]
        for s in range(TILES):
            value = (minus if s >= 4 else plus)(even[s % 4], odd[s % 4])
            value = times(times(value, angle, True), column(page_ref, rows, 2 * s), True)
            for part in range(2):
                at = slice(part * LANES + kappa, part * LANES + kappa + CHUNK), slice(q * LANES, (q + 1) * LANES)
                high_ref[s, *at], low_ref[s, *at] = split(value[part])
    for s in range(TILES):
        d_ref[s] = left_product(matrix_ref, 0, high_ref[s], low_ref[s])
    for chunk in range(LANES // CHUNK):
        rows = slice(chunk * CHUNK, (chunk + 1) * CHUNK)
        mix = mixes(page_ref, 0, rows, 16)
        for owner, out_ref in ((core, mine_ref), (1 - core, other_ref)):
            for t in range(4):
                s = 4 * owner + t
                v = [
                    d_ref[s, part * LANES + rows.start : part * LANES + rows.stop, q * LANES : (q + 1) * LANES]
                    for q in range(2)
                    for part in range(2)
                ]
                for a in range(4):
                    value = mixed(mix[4 * a : 4 * a + 4], v)
                    out_ref[pl.ds((a * LANES + rows.start) * 4 + t, CHUNK, stride=4), :] = value


VMEM_LIMIT = 32 * 1024 * 1024
VMEM_ALL = 60 * 1024 * 1024
FILTER_FLOPS = 3 * 2 * 256 * 256 * 256 * 16


def whole(s):
    return pl.BlockSpec(s.shape, lambda *_, n=len(s.shape): (0,) * n)


def call(kernel, out_shapes, args, in_specs=None, scratch=(), prefetch=0, flops=0, limit=VMEM_LIMIT):
    nbytes = sum(a.size * a.dtype.itemsize for a in args) + sum(int(np.prod(s.shape)) * 4 for s in out_shapes)
    single = len(out_shapes) == 1
    out_specs = [whole(s) for s in out_shapes]
    return pl.pallas_call(
        kernel,
        out_shape=out_shapes[0] if single else out_shapes,
        grid_spec=pltpu.PrefetchScalarGridSpec(
            num_scalar_prefetch=prefetch,
            grid=(1,),
            in_specs=in_specs or [whole(a) for a in args[prefetch:]],
            out_specs=out_specs[0] if single else out_specs,
            scratch_shapes=list(scratch),
        ),
        compiler_params=pltpu.CompilerParams(vmem_limit_bytes=limit),
        cost_estimate=pl.CostEstimate(flops=flops, bytes_accessed=nbytes, transcendentals=0),
    )(*args)


def shape(*dims):
    return jax.ShapeDtypeStruct(dims, F32)


HBM = pl.BlockSpec(memory_space=pltpu.HBM)


def stay(x):
    return pltpu.with_memory_space_constraint(x, pltpu.HBM)


def work(count):
    return [pltpu.VMEM((count, Q, Q), BF)] * 2


def tie_kernel(rows_ref, _, out_ref):
    pass


def after(rows, other):
    return pl.pallas_call(
        tie_kernel,
        out_shape=shape(*rows.shape),
        grid=(1,),
        in_specs=[pl.BlockSpec(memory_space=pl.ANY), whole(other)],
        out_specs=pl.BlockSpec(memory_space=pl.ANY),
        input_output_aliases={0: 0},
        compiler_params=pltpu.CompilerParams(vmem_limit_bytes=VMEM_LIMIT),
    )(rows, other)


def across(rows, mask):
    size = lax.axis_size("seq")
    return lax.ppermute(rows, "seq", [(i, i ^ mask) for i in range(size)])


def local(queries, keys, values, short_taps, long_filter, skip_gain):
    everyone = ("seq", "chan")
    size = lax.axis_size(everyone)
    seq_size = lax.axis_size("seq")
    me = (lax.axis_index("seq") % GROUP).astype(jnp.int32).reshape(1)
    channels = queries.shape[0]

    held = [pltpu.VMEM((4, 16, 2 * COLS), F32), pltpu.SemaphoreType.DMA((4,))]
    filter_rows = call(pack_filter_kernel, [shape(2 * ROWS, LANES)], (long_filter,), [HBM], held, limit=VMEM_ALL)
    alike = [list(range(member, seq_size, GROUP)) for member in range(GROUP)]
    filter_rows = lax.all_to_all(
        filter_rows.reshape(16, 64, LANES), "seq", 0, 0, tiled=True, axis_index_groups=alike
    ).reshape(2 * ROWS, LANES)

    edges = jnp.stack((queries[:, -2], queries[:, -1], keys[:, -2], keys[:, -1], values[:, -2], values[:, -1]))
    before = lax.ppermute(edges, everyone, [(i, i + 1) for i in range(size - 1)])
    small = jnp.concatenate((short_taps.reshape(9, channels), skip_gain[None], before)).T
    outs = [shape(2 * ROWS, LANES), shape(channels, COLS), shape(8, 16)]
    packed, drive, token = call(drive_kernel, outs, (keys, values, small))
    filter_rows = after(filter_rows, token)
    filter_far = across(filter_rows, 2)
    own = lax.all_to_all(packed.reshape(size, -1, LANES), everyone, 0, 0, tiled=True).reshape(2 * ROWS, LANES)

    flops = 3 * 2 * 256 * 256 * 256 * 8
    pieces = tuple(map(stay, (filter_rows, across(filter_rows, 1), filter_far, across(filter_far, 1))))
    matrices, pages = (stay(jnp.asarray(t)) for t in tables())
    page, table = shape(PAGE, LANES), jax.ShapeDtypeStruct(matrices.shape, BF)
    vmem = lambda s: pltpu.VMEM(s.shape, s.dtype)
    f32 = lambda *dims: pltpu.VMEM(dims, F32)
    sems = lambda count: pltpu.SemaphoreType.DMA((count,))
    spectrum = call(
        filter_kernel,
        [shape(TILES, Q, Q)],
        (me, pages, matrices, *pieces),
        [HBM] * 6,
        [vmem(page), vmem(table), sems(6), f32(GROUP, 2 * ROWS, LANES), f32(TILES, ROWS, LANES), f32(TILES, 2, Q, LANES)]
        + work(TILES),
        1,
        FILTER_FLOPS,
        VMEM_ALL,
    )
    mine, other, *loaded = call(
        drive_outer_kernel,
        [shape(2, 2, Q, LANES), shape(2, 2, Q, LANES), page, table, shape(TILES, Q, Q)],
        (me, pages, matrices, own, stay(spectrum)),
        [HBM, HBM, whole(own), HBM],
        [f32(2 * LANES, LANES), pltpu.VMEM((2, Q, Q), BF), sems(5), f32(2, ROWS, LANES)] + work(2),
        1,
        flops,
    )
    mine, other = call(
        product_kernel,
        [shape(4 * ROWS, LANES)] * 2,
        (me, mine, across(other, 1), *loaded),
        None,
        [f32(4, 2, Q, LANES), f32(TILES, Q, Q)] + work(TILES),
        1,
        3 * flops,
    )
    result = mine + across(other, 1)
    gain, direct = call(gate_kernel, [shape(channels, COLS)] * 2, (queries, drive, small))
    returned = lax.all_to_all(result.reshape(size, -1, LANES), everyone, 0, 0, tiled=True).reshape(4 * ROWS, LANES)
    return call(finish_kernel, [shape(channels, COLS)], (returned, gain, direct))


def solution(mesh):
    spread = P(None, ("seq", "chan"))
    in_specs = (spread, spread, spread, P(), P("chan", "seq"), P())
    return jax.shard_map(local, mesh=mesh, in_specs=in_specs, out_specs=spread, check_vma=False)
```

```python
import functools

import jax
import jax.numpy as jnp
import numpy as np
from jax import lax
from jax.experimental import pallas as pl
from jax.experimental.pallas import tpu as pltpu
from jax.sharding import PartitionSpec as P


BF = jnp.bfloat16
F32 = jnp.float32
GROUP = 4
ROWS = 512
COLS = 1024
Q = 256
LANES = 128
TILES = 8
CHUNK = 16
TOTAL = ROWS * COLS
ROOT = float(np.sqrt(0.5))


def halves(values):
    high = np.asarray(values, np.float32).astype(jnp.bfloat16)
    low = (np.asarray(values, np.float64) - high.astype(np.float64)).astype(np.float32).astype(jnp.bfloat16)
    return high, low


@functools.lru_cache(maxsize=None)
def tables():
    i = np.arange(LANES, dtype=np.float64)
    grid = 2.0 * np.pi * np.outer(i, i) / LANES
    cos, sin = np.cos(grid), np.sin(grid)
    ahead = np.block([[cos, -sin], [sin, cos]])
    matrices = np.stack((*halves(ahead), *halves(ahead.T)))
    steps = np.zeros((2, 2 * TILES, LANES))
    for r in range(TILES):
        angle = 2.0 * np.pi * r * i / COLS
        for chip in range(2):
            sign = -1.0 if chip and r % 2 else 1.0
            steps[chip, 2 * r], steps[chip, 2 * r + 1] = sign * np.cos(angle), -sign * np.sin(angle)
    turns = np.zeros((2, 2, Q, LANES))
    columns = np.zeros((GROUP, Q, LANES))
    mixes = np.zeros((2, LANES, LANES))
    for member in range(GROUP):
        chip, core = divmod(member, 2)
        k1 = np.concatenate((4.0 * i + core, 4.0 * i + 2.0 + core)) + 0.25
        angle = 2.0 * np.pi * np.outer(k1, i) / TOTAL
        turns[core, 0], turns[core, 1] = np.cos(angle), -np.sin(angle)
        for s in range(TILES):
            angle = 2.0 * np.pi * s * LANES * k1 / TOTAL
            columns[member, :, 2 * s], columns[member, :, 2 * s + 1] = np.cos(angle), -np.sin(angle)
        columns[member, :, 16:24] = columns[member, :, 8 * chip : 8 * chip + 8]
        for a in range(4):
            for q in range(2):
                angle = 2.0 * np.pi * (a * LANES + i) * (2.0 * q + core + 0.25) / ROWS
                at = 4 * a + 2 * q
                mixes[core, :, at], mixes[core, :, at + 1] = np.cos(angle), -np.sin(angle)
                mixes[core, :, 16 + at], mixes[core, :, 17 + at] = np.cos(angle) / TOTAL, -np.sin(angle) / TOTAL
    pages = []
    for member in range(GROUP):
        chip, core = divmod(member, 2)
        pages.append(
            np.concatenate((columns[member], turns[core, 0], turns[core, 1], mixes[core], mixes[1 - core], steps[chip], steps[0]))
        )
    return matrices, np.stack(pages).astype(np.float32)


def split(x):
    high = x.astype(BF)
    return high, (x - high.astype(F32)).astype(BF)


def mm(a, b):
    return jnp.dot(a, b, preferred_element_type=F32)


def pack_filter_kernel(filter_rows, out, held_ref, packed_ref, sem_ref):
    width = filter_rows.shape[1] // 4
    tiles = width // LANES
    ins = [(filter_rows.at[:, pl.ds(n * width, width)], held_ref.at[n]) for n in range(4)]
    loads = Loads(sem_ref.at[pl.ds(0, 4)], ins)
    stores = []
    for n in range(4):
        loads.wait(n)
        for tile in range(tiles):
            packed_ref[n, pl.ds(tile, 16, stride=tiles), :] = held_ref[n, :, tile * LANES : (tile + 1) * LANES]
        piece = packed_ref.at[n].reshape(16, tiles, LANES)
        stores.append(Loads(sem_ref.at[pl.ds(4 + n, 1)], [(piece, out.at[:, pl.ds(n * tiles, tiles), :])]))
    for store in stores:
        store.wait(0)


def feature(signal, taps, older, newer):
    lane = lax.broadcasted_iota(jnp.int32, signal.shape, 1)
    one = jnp.where(lane == 0, newer, pltpu.roll(signal, 1, 1))
    two = jnp.where(lane == 0, older, jnp.where(lane == 1, newer, pltpu.roll(signal, 2, 1)))
    return taps[0] * signal + taps[1] * one + taps[2] * two


def drive_kernel(keys_ref, values_ref, small_ref, packed_ref, drive_ref, token_ref):
    token_ref[...] = small_ref[:8, :16]
    for chan in range(8):
        rows = slice(16 * chan, 16 * chan + 16)
        col = lambda n: small_ref[rows, n : n + 1]
        key = feature(keys_ref[rows, :], [col(3), col(4), col(5)], col(12), col(13))
        value = feature(values_ref[rows, :], [col(6), col(7), col(8)], col(14), col(15))
        drive = key * value
        drive_ref[rows, :] = drive
        for member in range(GROUP):
            for half in range(2):
                at = (2 * member + half) * LANES
                packed_ref[pl.ds(16 * member + 2 * chan + half, 16, stride=64), :] = drive[:, at : at + LANES]


def gate_kernel(queries_ref, drive_ref, small_ref, gain_ref, direct_ref):
    for chan in range(8):
        rows = slice(16 * chan, 16 * chan + 16)
        col = lambda n: small_ref[rows, n : n + 1]
        query = feature(queries_ref[rows, :], [col(0), col(1), col(2)], col(10), col(11))
        gain_ref[rows, :] = query
        direct_ref[rows, :] = query * (col(9) * drive_ref[rows, :])


def finish_kernel(rows_ref, gain_ref, direct_ref, out_ref):
    for chan in range(8):
        rows = slice(16 * chan, 16 * chan + 16)
        for core in range(2):
            for tile in range(4):
                at = (4 * core + tile) * LANES
                first = rows_ref[pl.ds(32 * core + 4 * chan + tile, 16, stride=128), :]
                second = rows_ref[pl.ds(32 * (2 + core) + 4 * chan + tile, 16, stride=128), :]
                out_ref[rows, at : at + LANES] = (
                    gain_ref[rows, at : at + LANES] * (first + second) + direct_ref[rows, at : at + LANES]
                )


def times(a, b, conjugate=False):
    (ar, ai), (br, bi) = a, b
    if conjugate:
        return ar * br + ai * bi, ai * br - ar * bi
    return ar * br - ai * bi, ar * bi + ai * br


def mixed(weights, values):
    (w0, w1, w2, w3), (v0, v1, v2, v3) = weights, values
    return (w0 * v0 + w1 * v1) + (w2 * v2 + w3 * v3)


def plus(a, b):
    return a[0] + b[0], a[1] + b[1]


def minus(a, b):
    return a[0] - b[0], a[1] - b[1]


def turned(a, sign):
    return (-a[1], a[0]) if sign > 0 else (a[1], -a[0])


def eighth(a, power, sign):
    if power >= 2:
        a = turned(a, sign)
    if power % 2:
        real, imag = a
        a = ((real - sign * imag) * ROOT, (imag + sign * real) * ROOT)
    return a


def four(parts, sign):
    e, f = plus(parts[0], parts[2]), minus(parts[0], parts[2])
    g, h = plus(parts[1], parts[3]), turned(minus(parts[1], parts[3]), sign)
    return [plus(e, g), plus(f, h), minus(e, g), minus(f, h)]


TURN, MIX, STEP, PAGE = Q, 3 * Q, 4 * Q, 4 * Q + 4 * TILES


def column(page_ref, rows, n):
    return page_ref[rows, n : n + 1], page_ref[rows, n + 1 : n + 2]


def turn(page_ref, rows):
    return tuple(page_ref[TURN + part * Q + rows.start : TURN + part * Q + rows.stop, :] for part in range(2))


def mixes(page_ref, other, rows, first, base=MIX):
    at = base + other * LANES
    return [page_ref[at + rows.start : at + rows.stop, n : n + 1] for n in range(first, first + 16)]


def step(page_ref, plain, r):
    at = STEP + plain * 2 * TILES + 2 * r
    return page_ref[at : at + 1, :], page_ref[at + 1 : at + 2, :]


class Loads:
    def __init__(self, sem_ref, pairs):
        self.copies = [pltpu.make_async_copy(src, dst, sem_ref.at[n]) for n, (src, dst) in enumerate(pairs)]
        for copy in self.copies:
            copy.start()

    def wait(self, *which):
        for n in which:
            self.copies[n].wait()


def matrix(ref, transposed, axis):
    high, low = ref[2 * transposed], ref[2 * transposed + 1]
    return jnp.concatenate((high, high, low), axis)


def left_product(matrix_ref, transposed, high, low):
    return mm(matrix(matrix_ref, transposed, 1), jnp.concatenate((high, low, high), 0))


def right_product(matrix_ref, transposed, high, low):
    return mm(jnp.concatenate((high, low, high), 1), matrix(matrix_ref, transposed, 0))


def outer_transform(x_ref, count, other, page_ref, base, matrix_ref, transposed, f_ref, high_ref, low_ref):
    for chunk in range(LANES // CHUNK):
        rows = slice(chunk * CHUNK, (chunk + 1) * CHUNK)
        mix = mixes(page_ref, other, rows, 0, base)
        for s in range(count):
            x = [x_ref[s, a * LANES + rows.start : a * LANES + rows.stop, :] for a in range(4)]
            for q in range(2):
                for part in range(2):
                    u = mixed([mix[4 * a + 2 * q + part] for a in range(4)], x)
                    at = slice(part * LANES + rows.start, part * LANES + rows.stop), slice(q * LANES, (q + 1) * LANES)
                    high_ref[s, *at], low_ref[s, *at] = split(u)
    for s in range(count):
        result = left_product(matrix_ref, transposed, high_ref[s], low_ref[s])
        for part in range(2):
            for q in range(2):
                f_ref[s, part, q * LANES : (q + 1) * LANES, :] = result[
                    part * LANES : (part + 1) * LANES, q * LANES : (q + 1) * LANES
                ]


def inner_transform(f_ref, count, plain, first, page_ref, high_ref, low_ref):
    for chunk in range(Q // CHUNK):
        rows = slice(chunk * CHUNK, (chunk + 1) * CHUNK)
        angle = turn(page_ref, rows)
        parts = [
            times(times((f_ref[s, 0, rows, :], f_ref[s, 1, rows, :]), angle), column(page_ref, rows, first + 2 * s))
            for s in range(count)
        ]
        if count == TILES:
            even = [plus(parts[s], parts[s + 4]) for s in range(4)]
            odd = [minus(parts[s], parts[s + 4]) for s in range(4)]
        else:
            even = odd = parts
        even, odd = four(even, -1), four([eighth(odd[s], s, -1) for s in range(4)], -1)
        for r in range(TILES):
            value = (odd if r % 2 else even)[r // 2]
            if r:
                value = times(value, step(page_ref, plain, r))
            for part in range(2):
                at = rows, slice(part * LANES, (part + 1) * LANES)
                high_ref[r, *at], low_ref[r, *at] = split(value[part])


def filter_kernel(
    me_ref, pages, matrices, p0, p1, p2, p3, out_ref, page_ref, matrix_ref, sem_ref, held_ref, x_ref, f_ref, high_ref, low_ref
):
    me = me_ref[0]
    pieces = [(piece, held_ref.at[mask]) for mask, piece in enumerate((p0, p1, p2, p3))]
    loads = Loads(sem_ref, [(pages.at[me], page_ref), (matrices, matrix_ref), *pieces])
    for mask in range(GROUP):
        loads.wait(2 + mask)
        at = (me ^ mask) * 8
        for a in range(16):
            for tile in range(TILES):
                rows = pl.ds(pl.multiple_of(a * 32 + at, 8), 8)
                x_ref[tile, rows, :] = held_ref[mask, pl.ds(a * 64 + tile, 8, stride=8), :]
    loads.wait(0, 1)
    outer_transform(x_ref, TILES, 0, page_ref, MIX, matrix_ref, 1, f_ref, high_ref, low_ref)
    inner_transform(f_ref, TILES, 1, 0, page_ref, high_ref, low_ref)
    for r in range(TILES):
        out_ref[r] = right_product(matrix_ref, 0, high_ref[r], low_ref[r])


def drive_tiles(own_ref, x_ref):
    for half in range(2):
        x_ref[half] = own_ref[pl.ds(half, ROWS, stride=2), :]


def drive_other_kernel(me_ref, pages, matrices, own_ref, _, other_ref, mix_ref, ahead_ref, sem_ref, x_ref, high_ref, low_ref):
    mix, ahead = pages.at[me_ref[0], pl.ds(MIX, 2 * LANES)], matrices.at[pl.ds(2, 2)]
    loads = Loads(sem_ref, [(mix, mix_ref), (ahead, ahead_ref)])
    drive_tiles(own_ref, x_ref)
    loads.wait(0, 1)
    outer_transform(x_ref, 2, 1, mix_ref, 0, ahead_ref, 0, other_ref, high_ref, low_ref)


def drive_mine_kernel(
    me_ref, pages, matrices, own_ref, mix_ref, ahead_ref, mine_ref, page_ref, matrix_ref, sem_ref, x_ref, high_ref, low_ref
):
    loads = Loads(sem_ref, [(pages.at[me_ref[0]], page_ref), (matrices, matrix_ref)])
    drive_tiles(own_ref, x_ref)
    outer_transform(x_ref, 2, 0, mix_ref, 0, ahead_ref, 0, mine_ref, high_ref, low_ref)
    loads.wait(0, 1)


def product_kernel(
    me_ref,
    own_ref,
    peer_ref,
    page_ref,
    matrix_ref,
    spectrum,
    other_ref,
    left_high_ref,
    left_low_ref,
    sem_ref,
    filter_ref,
    f_ref,
    d_ref,
    high_ref,
    low_ref,
):
    core = me_ref[0] & 1
    loads = Loads(sem_ref, [(spectrum, filter_ref)])
    for which, piece_ref in ((core, own_ref), (1 - core, peer_ref)):
        for half in range(2):
            f_ref[2 * which + half] = piece_ref[half]
    inner_transform(f_ref, 4, 0, 16, page_ref, high_ref, low_ref)
    loads.wait(0)
    for r in range(TILES):
        x, h = right_product(matrix_ref, 0, high_ref[r], low_ref[r]), filter_ref[r]
        value = times((x[:, :LANES], x[:, LANES:]), (h[:, :LANES], h[:, LANES:]))
        d_ref[r] = right_product(matrix_ref, 1, *split(jnp.concatenate(value, 1)))
    for chunk in range(Q // CHUNK):
        rows = slice(chunk * CHUNK, (chunk + 1) * CHUNK)
        q, kappa = divmod(chunk * CHUNK, LANES)
        angle = turn(page_ref, rows)
        parts = []
        for r in range(TILES):
            value = d_ref[r, rows, :LANES], d_ref[r, rows, LANES:]
            if r:
                value = times(value, step(page_ref, 1, r), True)
            parts.append(value)
        even, odd = four(parts[0::2], 1), four(parts[1::2], 1)
        odd = [eighth(odd[s], s, 1) for s in range(4)]
        for s in range(TILES):
            value = (minus if s >= 4 else plus)(even[s % 4], odd[s % 4])
            value = times(times(value, angle, True), column(page_ref, rows, 2 * s), True)
            for part in range(2):
                at = slice(part * LANES + kappa, part * LANES + kappa + CHUNK), slice(q * LANES, (q + 1) * LANES)
                high_ref[s, *at], low_ref[s, *at] = split(value[part])
    for t in range(4):
        left_high_ref[t] = high_ref[4 * core + t]
        left_low_ref[t] = low_ref[4 * core + t]
        high, low = high_ref[4 * (1 - core) + t], low_ref[4 * (1 - core) + t]
        d_ref[t] = left_product(matrix_ref, 0, high, low)
    blend(d_ref, page_ref, other_ref)


def blend(d_ref, page_ref, out_ref):
    for chunk in range(LANES // CHUNK):
        rows = slice(chunk * CHUNK, (chunk + 1) * CHUNK)
        mix = mixes(page_ref, 0, rows, 16)
        for t in range(4):
            v = [
                d_ref[t, part * LANES + rows.start : part * LANES + rows.stop, q * LANES : (q + 1) * LANES]
                for q in range(2)
                for part in range(2)
            ]
            for a in range(4):
                value = mixed(mix[4 * a : 4 * a + 4], v)
                out_ref[pl.ds((a * LANES + rows.start) * 4 + t, CHUNK, stride=4), :] = value


def mine_kernel(high_ref, low_ref, page_ref, matrix_ref, out_ref, d_ref):
    for t in range(4):
        d_ref[t] = left_product(matrix_ref, 0, high_ref[t], low_ref[t])
    blend(d_ref, page_ref, out_ref)


VMEM_LIMIT = 32 * 1024 * 1024
VMEM_ALL = 60 * 1024 * 1024
FILTER_FLOPS = 3 * 2 * 256 * 256 * 256 * 16


def whole(s):
    return pl.BlockSpec(s.shape, lambda *_, n=len(s.shape): (0,) * n)


def call(kernel, out_shapes, args, in_specs=None, scratch=(), prefetch=0, flops=0, limit=VMEM_LIMIT, out_specs=None):
    nbytes = sum(a.size * a.dtype.itemsize for a in args) + sum(int(np.prod(s.shape)) * 4 for s in out_shapes)
    single = len(out_shapes) == 1
    out_specs = out_specs or [whole(s) for s in out_shapes]
    return pl.pallas_call(
        kernel,
        out_shape=out_shapes[0] if single else out_shapes,
        grid_spec=pltpu.PrefetchScalarGridSpec(
            num_scalar_prefetch=prefetch,
            grid=(1,),
            in_specs=in_specs or [whole(a) for a in args[prefetch:]],
            out_specs=out_specs[0] if single else out_specs,
            scratch_shapes=list(scratch),
        ),
        compiler_params=pltpu.CompilerParams(vmem_limit_bytes=limit),
        cost_estimate=pl.CostEstimate(flops=flops, bytes_accessed=nbytes, transcendentals=0),
    )(*args)


def shape(*dims):
    return jax.ShapeDtypeStruct(dims, F32)


HBM = pl.BlockSpec(memory_space=pltpu.HBM)


def stay(x):
    return pltpu.with_memory_space_constraint(x, pltpu.HBM)


def work(count):
    return [pltpu.VMEM((count, Q, Q), BF)] * 2


def tie_kernel(rows_ref, _, out_ref):
    pass


def after(rows, other):
    return pl.pallas_call(
        tie_kernel,
        out_shape=shape(*rows.shape),
        grid=(1,),
        in_specs=[pl.BlockSpec(memory_space=pl.ANY), whole(other)],
        out_specs=pl.BlockSpec(memory_space=pl.ANY),
        input_output_aliases={0: 0},
        compiler_params=pltpu.CompilerParams(vmem_limit_bytes=VMEM_LIMIT),
    )(rows, other)


def across(rows, mask):
    size = lax.axis_size("seq")
    return lax.ppermute(rows, "seq", [(i, i ^ mask) for i in range(size)])


def local(queries, keys, values, short_taps, long_filter, skip_gain):
    everyone = ("seq", "chan")
    size = lax.axis_size(everyone)
    seq_size = lax.axis_size("seq")
    me = (lax.axis_index("seq") % GROUP).astype(jnp.int32).reshape(1)
    channels = queries.shape[0]

    held = [pltpu.VMEM((4, 16, 2 * COLS), F32), pltpu.VMEM((4, 2 * LANES, LANES), F32), pltpu.SemaphoreType.DMA((8,))]
    filter_rows = call(pack_filter_kernel, [shape(16, 64, LANES)], (long_filter,), [HBM], held, limit=VMEM_ALL, out_specs=[HBM])
    alike = [list(range(member, seq_size, GROUP)) for member in range(GROUP)]
    filter_rows = lax.all_to_all(
        filter_rows, "seq", 0, 0, tiled=True, axis_index_groups=alike
    ).reshape(2 * ROWS, LANES)

    edges = jnp.stack((queries[:, -2], queries[:, -1], keys[:, -2], keys[:, -1], values[:, -2], values[:, -1]))
    before = lax.ppermute(edges, everyone, [(i, i + 1) for i in range(size - 1)])
    small = jnp.concatenate((short_taps.reshape(9, channels), skip_gain[None], before)).T
    outs = [shape(2 * ROWS, LANES), shape(channels, COLS), shape(8, 16)]
    packed, drive, token = call(drive_kernel, outs, (keys, values, small))
    filter_rows = after(filter_rows, token)
    filter_far = across(filter_rows, 2)
    own = lax.all_to_all(packed.reshape(size, -1, LANES), everyone, 0, 0, tiled=True).reshape(2 * ROWS, LANES)

    flops = 3 * 2 * 256 * 256 * 256 * 8
    pieces = tuple(map(stay, (filter_rows, across(filter_rows, 1), filter_far, across(filter_far, 1))))
    matrices, pages = (stay(jnp.asarray(t)) for t in tables())
    page, table = shape(PAGE, LANES), jax.ShapeDtypeStruct(matrices.shape, BF)
    vmem = lambda s: pltpu.VMEM(s.shape, s.dtype)
    f32 = lambda *dims: pltpu.VMEM(dims, F32)
    sems = lambda count: pltpu.SemaphoreType.DMA((count,))
    spectrum = call(
        filter_kernel,
        [shape(TILES, Q, Q)],
        (me, pages, matrices, *pieces),
        [HBM] * 6,
        [vmem(page), vmem(table), sems(6), f32(GROUP, 2 * ROWS, LANES), f32(TILES, ROWS, LANES), f32(TILES, 2, Q, LANES)]
        + work(TILES),
        1,
        FILTER_FLOPS,
        VMEM_ALL,
    )
    half, mix, ahead = shape(2, 2, Q, LANES), shape(2 * LANES, LANES), jax.ShapeDtypeStruct((2, Q, Q), BF)
    spectrum = stay(spectrum)
    other, mix, ahead = call(
        drive_other_kernel,
        [half, mix, ahead],
        (me, pages, matrices, own, spectrum),
        [HBM, HBM, whole(own), HBM],
        [sems(2), f32(2, ROWS, LANES)] + work(2),
        1,
        flops // 2,
    )
    mine, page, table = call(
        drive_mine_kernel,
        [half, page, table],
        (me, pages, matrices, own, mix, ahead),
        [HBM, HBM, whole(own), whole(mix), whole(ahead)],
        [sems(2), f32(2, ROWS, LANES)] + work(2),
        1,
        flops // 2,
    )
    peer = across(other, 1)
    left = jax.ShapeDtypeStruct((4, Q, Q), BF)
    other, *left = call(
        product_kernel,
        [shape(4 * ROWS, LANES), left, left],
        (me, mine, peer, page, table, spectrum),
        [whole(mine), whole(peer), whole(page), whole(table), HBM],
        [sems(1), f32(TILES, Q, Q), f32(4, 2, Q, LANES), f32(TILES, Q, Q)] + work(TILES),
        1,
        3 * flops,
    )
    mine = call(mine_kernel, [shape(4 * ROWS, LANES)], (*left, page, table), None, [f32(4, Q, Q)], 0, flops)
    result = mine + across(other, 1)
    gain, direct = call(gate_kernel, [shape(channels, COLS)] * 2, (queries, drive, small))
    returned = lax.all_to_all(result.reshape(size, -1, LANES), everyone, 0, 0, tiled=True).reshape(4 * ROWS, LANES)
    return call(finish_kernel, [shape(channels, COLS)], (returned, gain, direct))


def solution(mesh):
    spread = P(None, ("seq", "chan"))
    in_specs = (spread, spread, spread, P(), P("chan", "seq"), P())
    return jax.shard_map(local, mesh=mesh, in_specs=in_specs, out_specs=spread, check_vma=False)
```

```python
import functools

import jax
import jax.numpy as jnp
import numpy as np
from jax import lax
from jax.experimental import pallas as pl
from jax.experimental.pallas import tpu as pltpu
from jax.sharding import PartitionSpec as P


BF = jnp.bfloat16
F32 = jnp.float32
GROUP = 4
ROWS = 512
COLS = 1024
Q = 256
LANES = 128
TILES = 8
CHUNK = 16
TOTAL = ROWS * COLS
ROOT = float(np.sqrt(0.5))


def halves(values):
    high = np.asarray(values, np.float32).astype(jnp.bfloat16)
    low = (np.asarray(values, np.float64) - high.astype(np.float64)).astype(np.float32).astype(jnp.bfloat16)
    return high, low


@functools.lru_cache(maxsize=None)
def tables():
    i = np.arange(LANES, dtype=np.float64)
    grid = 2.0 * np.pi * np.outer(i, i) / LANES
    cos, sin = np.cos(grid), np.sin(grid)
    ahead = np.block([[cos, -sin], [sin, cos]])
    matrices = np.stack((*halves(ahead), *halves(ahead.T)))
    steps = np.zeros((2, 2 * TILES, LANES))
    for r in range(TILES):
        angle = 2.0 * np.pi * r * i / COLS
        for chip in range(2):
            sign = -1.0 if chip and r % 2 else 1.0
            steps[chip, 2 * r], steps[chip, 2 * r + 1] = sign * np.cos(angle), -sign * np.sin(angle)
    turns = np.zeros((2, 2, Q, LANES))
    columns = np.zeros((GROUP, Q, LANES))
    mixes = np.zeros((2, LANES, LANES))
    for member in range(GROUP):
        chip, core = divmod(member, 2)
        k1 = np.concatenate((4.0 * i + core, 4.0 * i + 2.0 + core)) + 0.25
        angle = 2.0 * np.pi * np.outer(k1, i) / TOTAL
        turns[core, 0], turns[core, 1] = np.cos(angle), -np.sin(angle)
        for s in range(TILES):
            angle = 2.0 * np.pi * s * LANES * k1 / TOTAL
            columns[member, :, 2 * s], columns[member, :, 2 * s + 1] = np.cos(angle), -np.sin(angle)
        columns[member, :, 16:24] = columns[member, :, 8 * chip : 8 * chip + 8]
        for a in range(4):
            for q in range(2):
                angle = 2.0 * np.pi * (a * LANES + i) * (2.0 * q + core + 0.25) / ROWS
                at = 4 * a + 2 * q
                mixes[core, :, at], mixes[core, :, at + 1] = np.cos(angle), -np.sin(angle)
                mixes[core, :, 16 + at], mixes[core, :, 17 + at] = np.cos(angle) / TOTAL, -np.sin(angle) / TOTAL
    pages = []
    for member in range(GROUP):
        chip, core = divmod(member, 2)
        pages.append(
            np.concatenate((columns[member], turns[core, 0], turns[core, 1], mixes[core], mixes[1 - core], steps[chip], steps[0]))
        )
    return matrices, np.stack(pages).astype(np.float32)


def split(x):
    high = x.astype(BF)
    return high, (x - high.astype(F32)).astype(BF)


def mm(a, b):
    return jnp.dot(a, b, preferred_element_type=F32)


def pack_filter_kernel(filter_rows, out, held_ref, packed_ref, sem_ref):
    width = filter_rows.shape[1] // 4
    tiles = width // LANES
    ins = [(filter_rows.at[:, pl.ds(n * width, width)], held_ref.at[n]) for n in range(4)]
    loads = Loads(sem_ref.at[pl.ds(0, 4)], ins)
    stores = []
    for n in range(4):
        loads.wait(n)
        for tile in range(tiles):
            packed_ref[n, pl.ds(tile, 16, stride=tiles), :] = held_ref[n, :, tile * LANES : (tile + 1) * LANES]
        piece = packed_ref.at[n].reshape(16, tiles, LANES)
        stores.append(Loads(sem_ref.at[pl.ds(4 + n, 1)], [(piece, out.at[:, pl.ds(n * tiles, tiles), :])]))
    for store in stores:
        store.wait(0)


def feature(signal, taps, older, newer):
    lane = lax.broadcasted_iota(jnp.int32, signal.shape, 1)
    one = jnp.where(lane == 0, newer, pltpu.roll(signal, 1, 1))
    two = jnp.where(lane == 0, older, jnp.where(lane == 1, newer, pltpu.roll(signal, 2, 1)))
    return taps[0] * signal + taps[1] * one + taps[2] * two


def drive_kernel(keys_ref, values_ref, small_ref, packed_ref, drive_ref, token_ref):
    token_ref[...] = small_ref[:8, :16]
    for chan in range(8):
        rows = slice(16 * chan, 16 * chan + 16)
        col = lambda n: small_ref[rows, n : n + 1]
        key = feature(keys_ref[rows, :], [col(3), col(4), col(5)], col(12), col(13))
        value = feature(values_ref[rows, :], [col(6), col(7), col(8)], col(14), col(15))
        drive = key * value
        drive_ref[rows, :] = drive
        for member in range(GROUP):
            for half in range(2):
                at = (2 * member + half) * LANES
                packed_ref[pl.ds(16 * member + 2 * chan + half, 16, stride=64), :] = drive[:, at : at + LANES]


def gate_kernel(queries_ref, drive_ref, small_ref, gain_ref, direct_ref):
    for chan in range(8):
        rows = slice(16 * chan, 16 * chan + 16)
        col = lambda n: small_ref[rows, n : n + 1]
        query = feature(queries_ref[rows, :], [col(0), col(1), col(2)], col(10), col(11))
        gain_ref[rows, :] = query
        direct_ref[rows, :] = query * (col(9) * drive_ref[rows, :])


def finish_kernel(rows_ref, gain_ref, direct_ref, out_ref):
    for chan in range(8):
        rows = slice(16 * chan, 16 * chan + 16)
        for core in range(2):
            for tile in range(4):
                at = (4 * core + tile) * LANES
                first = rows_ref[pl.ds(32 * core + 4 * chan + tile, 16, stride=128), :]
                second = rows_ref[pl.ds(32 * (2 + core) + 4 * chan + tile, 16, stride=128), :]
                out_ref[rows, at : at + LANES] = (
                    gain_ref[rows, at : at + LANES] * (first + second) + direct_ref[rows, at : at + LANES]
                )


def times(a, b, conjugate=False):
    (ar, ai), (br, bi) = a, b
    if conjugate:
        return ar * br + ai * bi, ai * br - ar * bi
    return ar * br - ai * bi, ar * bi + ai * br


def mixed(weights, values):
    (w0, w1, w2, w3), (v0, v1, v2, v3) = weights, values
    return (w0 * v0 + w1 * v1) + (w2 * v2 + w3 * v3)


def plus(a, b):
    return a[0] + b[0], a[1] + b[1]


def minus(a, b):
    return a[0] - b[0], a[1] - b[1]


def turned(a, sign):
    return (-a[1], a[0]) if sign > 0 else (a[1], -a[0])


def eighth(a, power, sign):
    if power >= 2:
        a = turned(a, sign)
    if power % 2:
        real, imag = a
        a = ((real - sign * imag) * ROOT, (imag + sign * real) * ROOT)
    return a


def four(parts, sign):
    e, f = plus(parts[0], parts[2]), minus(parts[0], parts[2])
    g, h = plus(parts[1], parts[3]), turned(minus(parts[1], parts[3]), sign)
    return [plus(e, g), plus(f, h), minus(e, g), minus(f, h)]


TURN, MIX, STEP, PAGE = Q, 3 * Q, 4 * Q, 4 * Q + 4 * TILES


def column(page_ref, rows, n):
    return page_ref[rows, n : n + 1], page_ref[rows, n + 1 : n + 2]


def turn(page_ref, rows):
    return tuple(page_ref[TURN + part * Q + rows.start : TURN + part * Q + rows.stop, :] for part in range(2))


def mixes(page_ref, other, rows, first, base=MIX):
    at = base + other * LANES
    return [page_ref[at + rows.start : at + rows.stop, n : n + 1] for n in range(first, first + 16)]


def step(page_ref, plain, r):
    at = STEP + plain * 2 * TILES + 2 * r
    return page_ref[at : at + 1, :], page_ref[at + 1 : at + 2, :]


class Loads:
    def __init__(self, sem_ref, pairs):
        self.copies = [pltpu.make_async_copy(src, dst, sem_ref.at[n]) for n, (src, dst) in enumerate(pairs)]
        for copy in self.copies:
            copy.start()

    def wait(self, *which):
        for n in which:
            self.copies[n].wait()


def matrix(ref, transposed, axis):
    high, low = ref[2 * transposed], ref[2 * transposed + 1]
    return jnp.concatenate((high, high, low), axis)


def left_product(matrix_ref, transposed, high, low):
    return mm(matrix(matrix_ref, transposed, 1), jnp.concatenate((high, low, high), 0))


def right_product(matrix_ref, transposed, high, low):
    return mm(jnp.concatenate((high, low, high), 1), matrix(matrix_ref, transposed, 0))


def outer_transform(x_ref, count, other, page_ref, base, matrix_ref, transposed, f_ref, high_ref, low_ref):
    for chunk in range(LANES // CHUNK):
        rows = slice(chunk * CHUNK, (chunk + 1) * CHUNK)
        mix = mixes(page_ref, other, rows, 0, base)
        for s in range(count):
            x = [x_ref[s, a * LANES + rows.start : a * LANES + rows.stop, :] for a in range(4)]
            for q in range(2):
                for part in range(2):
                    u = mixed([mix[4 * a + 2 * q + part] for a in range(4)], x)
                    at = slice(part * LANES + rows.start, part * LANES + rows.stop), slice(q * LANES, (q + 1) * LANES)
                    high_ref[s, *at], low_ref[s, *at] = split(u)
    for s in range(count):
        result = left_product(matrix_ref, transposed, high_ref[s], low_ref[s])
        for part in range(2):
            for q in range(2):
                f_ref[s, part, q * LANES : (q + 1) * LANES, :] = result[
                    part * LANES : (part + 1) * LANES, q * LANES : (q + 1) * LANES
                ]


def inner_transform(f_ref, count, plain, first, page_ref, high_ref, low_ref):
    for chunk in range(Q // CHUNK):
        rows = slice(chunk * CHUNK, (chunk + 1) * CHUNK)
        angle = turn(page_ref, rows)
        parts = [
            times(times((f_ref[s, 0, rows, :], f_ref[s, 1, rows, :]), angle), column(page_ref, rows, first + 2 * s))
            for s in range(count)
        ]
        if count == TILES:
            even = [plus(parts[s], parts[s + 4]) for s in range(4)]
            odd = [minus(parts[s], parts[s + 4]) for s in range(4)]
        else:
            even = odd = parts
        even, odd = four(even, -1), four([eighth(odd[s], s, -1) for s in range(4)], -1)
        for r in range(TILES):
            value = (odd if r % 2 else even)[r // 2]
            if r:
                value = times(value, step(page_ref, plain, r))
            for part in range(2):
                at = rows, slice(part * LANES, (part + 1) * LANES)
                high_ref[r, *at], low_ref[r, *at] = split(value[part])


def filter_kernel(
    me_ref, pages, matrices, p0, p1, p2, p3, out_ref, page_ref, matrix_ref, sem_ref, held_ref, x_ref, f_ref, high_ref, low_ref
):
    me = me_ref[0]
    pieces = [(piece, held_ref.at[mask]) for mask, piece in enumerate((p0, p1, p2, p3))]
    loads = Loads(sem_ref, [(pages.at[me], page_ref), (matrices, matrix_ref), *pieces])
    for mask in range(GROUP):
        loads.wait(2 + mask)
        at = (me ^ mask) * 8
        for a in range(16):
            for tile in range(TILES):
                rows = pl.ds(pl.multiple_of(a * 32 + at, 8), 8)
                x_ref[tile, rows, :] = held_ref[mask, pl.ds(a * 64 + tile, 8, stride=8), :]
    loads.wait(0, 1)
    outer_transform(x_ref, TILES, 0, page_ref, MIX, matrix_ref, 1, f_ref, high_ref, low_ref)
    inner_transform(f_ref, TILES, 1, 0, page_ref, high_ref, low_ref)
    for r in range(TILES):
        out_ref[r] = right_product(matrix_ref, 0, high_ref[r], low_ref[r])


def drive_outer_kernel(
    me_ref,
    pages,
    matrices,
    own_ref,
    spectrum,
    mine_ref,
    other_ref,
    page_ref,
    matrix_ref,
    filter_ref,
    mix_ref,
    ahead_ref,
    sem_ref,
    x_ref,
    high_ref,
    low_ref,
):
    page = pages.at[me_ref[0]]
    first = [(page.at[pl.ds(MIX, 2 * LANES)], mix_ref), (matrices.at[pl.ds(2, 2)], ahead_ref)]
    loads = Loads(sem_ref, [*first, (page, page_ref), (matrices, matrix_ref), (spectrum, filter_ref)])
    for half in range(2):
        x_ref[half] = own_ref[pl.ds(half, ROWS, stride=2), :]
    loads.wait(0, 1)
    outer_transform(x_ref, 2, 1, mix_ref, 0, ahead_ref, 0, other_ref, high_ref, low_ref)
    outer_transform(x_ref, 2, 0, mix_ref, 0, ahead_ref, 0, mine_ref, high_ref, low_ref)
    loads.wait(2, 3, 4)


def product_kernel(
    me_ref,
    own_ref,
    peer_ref,
    page_ref,
    matrix_ref,
    filter_ref,
    other_ref,
    left_high_ref,
    left_low_ref,
    f_ref,
    d_ref,
    high_ref,
    low_ref,
):
    core = me_ref[0] & 1
    for which, piece_ref in ((core, own_ref), (1 - core, peer_ref)):
        for half in range(2):
            f_ref[2 * which + half] = piece_ref[half]
    inner_transform(f_ref, 4, 0, 16, page_ref, high_ref, low_ref)
    for r in range(TILES):
        x, h = right_product(matrix_ref, 0, high_ref[r], low_ref[r]), filter_ref[r]
        value = times((x[:, :LANES], x[:, LANES:]), (h[:, :LANES], h[:, LANES:]))
        d_ref[r] = right_product(matrix_ref, 1, *split(jnp.concatenate(value, 1)))
    for chunk in range(Q // CHUNK):
        rows = slice(chunk * CHUNK, (chunk + 1) * CHUNK)
        q, kappa = divmod(chunk * CHUNK, LANES)
        angle = turn(page_ref, rows)
        parts = []
        for r in range(TILES):
            value = d_ref[r, rows, :LANES], d_ref[r, rows, LANES:]
            if r:
                value = times(value, step(page_ref, 1, r), True)
            parts.append(value)
        even, odd = four(parts[0::2], 1), four(parts[1::2], 1)
        odd = [eighth(odd[s], s, 1) for s in range(4)]
        for s in range(TILES):
            value = (minus if s >= 4 else plus)(even[s % 4], odd[s % 4])
            value = times(times(value, angle, True), column(page_ref, rows, 2 * s), True)
            for part in range(2):
                at = slice(part * LANES + kappa, part * LANES + kappa + CHUNK), slice(q * LANES, (q + 1) * LANES)
                high_ref[s, *at], low_ref[s, *at] = split(value[part])
    for t in range(4):
        left_high_ref[t] = high_ref[4 * core + t]
        left_low_ref[t] = low_ref[4 * core + t]
        high, low = high_ref[4 * (1 - core) + t], low_ref[4 * (1 - core) + t]
        d_ref[t] = left_product(matrix_ref, 0, high, low)
    blend(d_ref, page_ref, other_ref)


def blend(d_ref, page_ref, out_ref):
    for chunk in range(LANES // CHUNK):
        rows = slice(chunk * CHUNK, (chunk + 1) * CHUNK)
        mix = mixes(page_ref, 0, rows, 16)
        for t in range(4):
            v = [
                d_ref[t, part * LANES + rows.start : part * LANES + rows.stop, q * LANES : (q + 1) * LANES]
                for q in range(2)
                for part in range(2)
            ]
            for a in range(4):
                value = mixed(mix[4 * a : 4 * a + 4], v)
                out_ref[pl.ds((a * LANES + rows.start) * 4 + t, CHUNK, stride=4), :] = value


def mine_kernel(high_ref, low_ref, page_ref, matrix_ref, out_ref, d_ref):
    for t in range(4):
        d_ref[t] = left_product(matrix_ref, 0, high_ref[t], low_ref[t])
    blend(d_ref, page_ref, out_ref)


VMEM_LIMIT = 32 * 1024 * 1024
VMEM_ALL = 60 * 1024 * 1024
FILTER_FLOPS = 3 * 2 * 256 * 256 * 256 * 16


def whole(s):
    return pl.BlockSpec(s.shape, lambda *_, n=len(s.shape): (0,) * n)


def call(kernel, out_shapes, args, in_specs=None, scratch=(), prefetch=0, flops=0, limit=VMEM_LIMIT, out_specs=None):
    nbytes = sum(a.size * a.dtype.itemsize for a in args) + sum(int(np.prod(s.shape)) * 4 for s in out_shapes)
    single = len(out_shapes) == 1
    out_specs = out_specs or [whole(s) for s in out_shapes]
    return pl.pallas_call(
        kernel,
        out_shape=out_shapes[0] if single else out_shapes,
        grid_spec=pltpu.PrefetchScalarGridSpec(
            num_scalar_prefetch=prefetch,
            grid=(1,),
            in_specs=in_specs or [whole(a) for a in args[prefetch:]],
            out_specs=out_specs[0] if single else out_specs,
            scratch_shapes=list(scratch),
        ),
        compiler_params=pltpu.CompilerParams(vmem_limit_bytes=limit),
        cost_estimate=pl.CostEstimate(flops=flops, bytes_accessed=nbytes, transcendentals=0),
    )(*args)


def shape(*dims):
    return jax.ShapeDtypeStruct(dims, F32)


HBM = pl.BlockSpec(memory_space=pltpu.HBM)


def stay(x):
    return pltpu.with_memory_space_constraint(x, pltpu.HBM)


def work(count):
    return [pltpu.VMEM((count, Q, Q), BF)] * 2


def tie_kernel(rows_ref, _, out_ref):
    pass


def after(rows, other):
    return pl.pallas_call(
        tie_kernel,
        out_shape=shape(*rows.shape),
        grid=(1,),
        in_specs=[pl.BlockSpec(memory_space=pl.ANY), whole(other)],
        out_specs=pl.BlockSpec(memory_space=pl.ANY),
        input_output_aliases={0: 0},
        compiler_params=pltpu.CompilerParams(vmem_limit_bytes=VMEM_LIMIT),
    )(rows, other)


def across(rows, mask):
    size = lax.axis_size("seq")
    return lax.ppermute(rows, "seq", [(i, i ^ mask) for i in range(size)])


def local(queries, keys, values, short_taps, long_filter, skip_gain):
    everyone = ("seq", "chan")
    size = lax.axis_size(everyone)
    seq_size = lax.axis_size("seq")
    me = (lax.axis_index("seq") % GROUP).astype(jnp.int32).reshape(1)
    channels = queries.shape[0]

    held = [pltpu.VMEM((4, 16, 2 * COLS), F32), pltpu.VMEM((4, 2 * LANES, LANES), F32), pltpu.SemaphoreType.DMA((8,))]
    filter_rows = call(pack_filter_kernel, [shape(16, 64, LANES)], (long_filter,), [HBM], held, limit=VMEM_ALL, out_specs=[HBM])
    alike = [list(range(member, seq_size, GROUP)) for member in range(GROUP)]
    filter_rows = lax.all_to_all(
        filter_rows, "seq", 0, 0, tiled=True, axis_index_groups=alike
    ).reshape(2 * ROWS, LANES)

    edges = jnp.stack((queries[:, -2], queries[:, -1], keys[:, -2], keys[:, -1], values[:, -2], values[:, -1]))
    before = lax.ppermute(edges, everyone, [(i, i + 1) for i in range(size - 1)])
    small = jnp.concatenate((short_taps.reshape(9, channels), skip_gain[None], before)).T
    outs = [shape(2 * ROWS, LANES), shape(channels, COLS), shape(8, 16)]
    packed, drive, token = call(drive_kernel, outs, (keys, values, small))
    filter_rows = after(filter_rows, token)
    filter_far = across(filter_rows, 2)
    own = lax.all_to_all(packed.reshape(size, -1, LANES), everyone, 0, 0, tiled=True).reshape(2 * ROWS, LANES)

    flops = 3 * 2 * 256 * 256 * 256 * 8
    pieces = tuple(map(stay, (filter_rows, across(filter_rows, 1), filter_far, across(filter_far, 1))))
    matrices, pages = (stay(jnp.asarray(t)) for t in tables())
    page, table = shape(PAGE, LANES), jax.ShapeDtypeStruct(matrices.shape, BF)
    vmem = lambda s: pltpu.VMEM(s.shape, s.dtype)
    f32 = lambda *dims: pltpu.VMEM(dims, F32)
    sems = lambda count: pltpu.SemaphoreType.DMA((count,))
    spectrum = call(
        filter_kernel,
        [shape(TILES, Q, Q)],
        (me, pages, matrices, *pieces),
        [HBM] * 6,
        [vmem(page), vmem(table), sems(6), f32(GROUP, 2 * ROWS, LANES), f32(TILES, ROWS, LANES), f32(TILES, 2, Q, LANES)]
        + work(TILES),
        1,
        FILTER_FLOPS,
        VMEM_ALL,
    )
    mine, other, *loaded = call(
        drive_outer_kernel,
        [shape(2, 2, Q, LANES), shape(2, 2, Q, LANES), page, table, shape(TILES, Q, Q)],
        (me, pages, matrices, own, stay(spectrum)),
        [HBM, HBM, whole(own), HBM],
        [f32(2 * LANES, LANES), pltpu.VMEM((2, Q, Q), BF), sems(5), f32(2, ROWS, LANES)] + work(2),
        1,
        flops,
    )
    left = jax.ShapeDtypeStruct((4, Q, Q), BF)
    page, table, _ = loaded
    other, *left = call(
        product_kernel,
        [shape(4 * ROWS, LANES), left, left],
        (me, mine, across(other, 1), *loaded),
        None,
        [f32(4, 2, Q, LANES), f32(TILES, Q, Q)] + work(TILES),
        1,
        3 * flops,
    )
    mine = call(mine_kernel, [shape(4 * ROWS, LANES)], (*left, page, table), None, [f32(4, Q, Q)], 0, flops)
    result = mine + across(other, 1)
    gain, direct = call(gate_kernel, [shape(channels, COLS)] * 2, (queries, drive, small))
    returned = lax.all_to_all(result.reshape(size, -1, LANES), everyone, 0, 0, tiled=True).reshape(4 * ROWS, LANES)
    return call(finish_kernel, [shape(channels, COLS)], (returned, gain, direct))


def solution(mesh):
    spread = P(None, ("seq", "chan"))
    in_specs = (spread, spread, spread, P(), P("chan", "seq"), P())
    return jax.shard_map(local, mesh=mesh, in_specs=in_specs, out_specs=spread, check_vma=False)
```

```python
import functools

import jax
import jax.numpy as jnp
import numpy as np
from jax import lax
from jax.experimental import pallas as pl
from jax.experimental.pallas import tpu as pltpu
from jax.sharding import PartitionSpec as P


BF = jnp.bfloat16
F32 = jnp.float32
GROUP = 4
ROWS = 512
COLS = 1024
Q = 256
LANES = 128
TILES = 8
CHUNK = 16
TOTAL = ROWS * COLS
ROOT = float(np.sqrt(0.5))


def halves(values):
    high = np.asarray(values, np.float32).astype(jnp.bfloat16)
    low = (np.asarray(values, np.float64) - high.astype(np.float64)).astype(np.float32).astype(jnp.bfloat16)
    return high, low


@functools.lru_cache(maxsize=None)
def tables():
    i = np.arange(LANES, dtype=np.float64)
    grid = 2.0 * np.pi * np.outer(i, i) / LANES
    cos, sin = np.cos(grid), np.sin(grid)
    ahead = np.block([[cos, -sin], [sin, cos]])
    matrices = np.stack((*halves(ahead), *halves(ahead.T)))
    steps = np.zeros((2, 2 * TILES, LANES))
    for r in range(TILES):
        angle = 2.0 * np.pi * r * i / COLS
        for chip in range(2):
            sign = -1.0 if chip and r % 2 else 1.0
            steps[chip, 2 * r], steps[chip, 2 * r + 1] = sign * np.cos(angle), -sign * np.sin(angle)
    turns = np.zeros((2, 2, Q, LANES))
    columns = np.zeros((GROUP, Q, LANES))
    mixes = np.zeros((2, LANES, LANES))
    for member in range(GROUP):
        chip, core = divmod(member, 2)
        k1 = np.concatenate((4.0 * i + core, 4.0 * i + 2.0 + core)) + 0.25
        angle = 2.0 * np.pi * np.outer(k1, i) / TOTAL
        turns[core, 0], turns[core, 1] = np.cos(angle), -np.sin(angle)
        for s in range(TILES):
            angle = 2.0 * np.pi * s * LANES * k1 / TOTAL
            columns[member, :, 2 * s], columns[member, :, 2 * s + 1] = np.cos(angle), -np.sin(angle)
        columns[member, :, 16:24] = columns[member, :, 8 * chip : 8 * chip + 8]
        for a in range(4):
            for q in range(2):
                angle = 2.0 * np.pi * (a * LANES + i) * (2.0 * q + core + 0.25) / ROWS
                at = 4 * a + 2 * q
                mixes[core, :, at], mixes[core, :, at + 1] = np.cos(angle), -np.sin(angle)
                mixes[core, :, 16 + at], mixes[core, :, 17 + at] = np.cos(angle) / TOTAL, -np.sin(angle) / TOTAL
    pages = []
    for member in range(GROUP):
        chip, core = divmod(member, 2)
        pages.append(
            np.concatenate((columns[member], turns[core, 0], turns[core, 1], mixes[core], mixes[1 - core], steps[chip], steps[0]))
        )
    return matrices, np.stack(pages).astype(np.float32)


def split(x):
    high = x.astype(BF)
    return high, (x - high.astype(F32)).astype(BF)


def mm(a, b):
    return jnp.dot(a, b, preferred_element_type=F32)


def pack_filter_kernel(filter_rows, out, held_ref, packed_ref, sem_ref):
    width = filter_rows.shape[1] // 4
    tiles = width // LANES
    ins = [(filter_rows.at[:, pl.ds(n * width, width)], held_ref.at[n]) for n in range(4)]
    loads = Loads(sem_ref.at[pl.ds(0, 4)], ins)
    stores = []
    for n in range(4):
        loads.wait(n)
        for tile in range(tiles):
            packed_ref[n, pl.ds(tile, 16, stride=tiles), :] = held_ref[n, :, tile * LANES : (tile + 1) * LANES]
        piece = packed_ref.at[n].reshape(16, tiles, LANES)
        stores.append(Loads(sem_ref.at[pl.ds(4 + n, 1)], [(piece, out.at[:, pl.ds(n * tiles, tiles), :])]))
    for store in stores:
        store.wait(0)


def feature(signal, taps, older, newer):
    lane = lax.broadcasted_iota(jnp.int32, signal.shape, 1)
    one = jnp.where(lane == 0, newer, pltpu.roll(signal, 1, 1))
    two = jnp.where(lane == 0, older, jnp.where(lane == 1, newer, pltpu.roll(signal, 2, 1)))
    return taps[0] * signal + taps[1] * one + taps[2] * two


def drive_kernel(keys_ref, values_ref, small_ref, packed_ref, drive_ref, token_ref):
    token_ref[...] = small_ref[:8, :16]
    for chan in range(8):
        rows = slice(16 * chan, 16 * chan + 16)
        col = lambda n: small_ref[rows, n : n + 1]
        key = feature(keys_ref[rows, :], [col(3), col(4), col(5)], col(12), col(13))
        value = feature(values_ref[rows, :], [col(6), col(7), col(8)], col(14), col(15))
        drive = key * value
        drive_ref[rows, :] = drive
        for member in range(GROUP):
            for half in range(2):
                at = (2 * member + half) * LANES
                packed_ref[pl.ds(16 * member + 2 * chan + half, 16, stride=64), :] = drive[:, at : at + LANES]


def gate_kernel(queries_ref, drive_ref, small_ref, gain_ref, direct_ref):
    for chan in range(8):
        rows = slice(16 * chan, 16 * chan + 16)
        col = lambda n: small_ref[rows, n : n + 1]
        query = feature(queries_ref[rows, :], [col(0), col(1), col(2)], col(10), col(11))
        gain_ref[rows, :] = query
        direct_ref[rows, :] = query * (col(9) * drive_ref[rows, :])


def finish_kernel(rows_ref, gain_ref, direct_ref, out_ref):
    for chan in range(8):
        rows = slice(16 * chan, 16 * chan + 16)
        for core in range(2):
            for tile in range(4):
                at = (4 * core + tile) * LANES
                first = rows_ref[pl.ds(32 * core + 4 * chan + tile, 16, stride=128), :]
                second = rows_ref[pl.ds(32 * (2 + core) + 4 * chan + tile, 16, stride=128), :]
                out_ref[rows, at : at + LANES] = (
                    gain_ref[rows, at : at + LANES] * (first + second) + direct_ref[rows, at : at + LANES]
                )


def times(a, b, conjugate=False):
    (ar, ai), (br, bi) = a, b
    if conjugate:
        return ar * br + ai * bi, ai * br - ar * bi
    return ar * br - ai * bi, ar * bi + ai * br


def mixed(weights, values):
    (w0, w1, w2, w3), (v0, v1, v2, v3) = weights, values
    return (w0 * v0 + w1 * v1) + (w2 * v2 + w3 * v3)


def plus(a, b):
    return a[0] + b[0], a[1] + b[1]


def minus(a, b):
    return a[0] - b[0], a[1] - b[1]


def turned(a, sign):
    return (-a[1], a[0]) if sign > 0 else (a[1], -a[0])


def eighth(a, power, sign):
    if power >= 2:
        a = turned(a, sign)
    if power % 2:
        real, imag = a
        a = ((real - sign * imag) * ROOT, (imag + sign * real) * ROOT)
    return a


def four(parts, sign):
    e, f = plus(parts[0], parts[2]), minus(parts[0], parts[2])
    g, h = plus(parts[1], parts[3]), turned(minus(parts[1], parts[3]), sign)
    return [plus(e, g), plus(f, h), minus(e, g), minus(f, h)]


TURN, MIX, STEP, PAGE = Q, 3 * Q, 4 * Q, 4 * Q + 4 * TILES


def column(page_ref, rows, n):
    return page_ref[rows, n : n + 1], page_ref[rows, n + 1 : n + 2]


def turn(page_ref, rows):
    return tuple(page_ref[TURN + part * Q + rows.start : TURN + part * Q + rows.stop, :] for part in range(2))


def mixes(page_ref, other, rows, first, base=MIX):
    at = base + other * LANES
    return [page_ref[at + rows.start : at + rows.stop, n : n + 1] for n in range(first, first + 16)]


def step(page_ref, plain, r):
    at = STEP + plain * 2 * TILES + 2 * r
    return page_ref[at : at + 1, :], page_ref[at + 1 : at + 2, :]


class Loads:
    def __init__(self, sem_ref, pairs):
        self.copies = [pltpu.make_async_copy(src, dst, sem_ref.at[n]) for n, (src, dst) in enumerate(pairs)]
        for copy in self.copies:
            copy.start()

    def wait(self, *which):
        for n in which:
            self.copies[n].wait()


def matrix(ref, transposed, axis):
    high, low = ref[2 * transposed], ref[2 * transposed + 1]
    return jnp.concatenate((high, high, low), axis)


def left_product(matrix_ref, transposed, high, low):
    return mm(matrix(matrix_ref, transposed, 1), jnp.concatenate((high, low, high), 0))


def right_product(matrix_ref, transposed, high, low):
    return mm(jnp.concatenate((high, low, high), 1), matrix(matrix_ref, transposed, 0))


def outer_transform(x_ref, count, other, page_ref, base, matrix_ref, transposed, f_ref, high_ref, low_ref):
    for chunk in range(LANES // CHUNK):
        rows = slice(chunk * CHUNK, (chunk + 1) * CHUNK)
        mix = mixes(page_ref, other, rows, 0, base)
        for s in range(count):
            x = [x_ref[s, a * LANES + rows.start : a * LANES + rows.stop, :] for a in range(4)]
            for q in range(2):
                for part in range(2):
                    u = mixed([mix[4 * a + 2 * q + part] for a in range(4)], x)
                    at = slice(part * LANES + rows.start, part * LANES + rows.stop), slice(q * LANES, (q + 1) * LANES)
                    high_ref[s, *at], low_ref[s, *at] = split(u)
    for s in range(count):
        result = left_product(matrix_ref, transposed, high_ref[s], low_ref[s])
        for part in range(2):
            for q in range(2):
                f_ref[s, part, q * LANES : (q + 1) * LANES, :] = result[
                    part * LANES : (part + 1) * LANES, q * LANES : (q + 1) * LANES
                ]


def inner_transform(f_ref, count, plain, first, page_ref, high_ref, low_ref):
    for chunk in range(Q // CHUNK):
        rows = slice(chunk * CHUNK, (chunk + 1) * CHUNK)
        angle = turn(page_ref, rows)
        parts = [
            times(times((f_ref[s, 0, rows, :], f_ref[s, 1, rows, :]), angle), column(page_ref, rows, first + 2 * s))
            for s in range(count)
        ]
        if count == TILES:
            even = [plus(parts[s], parts[s + 4]) for s in range(4)]
            odd = [minus(parts[s], parts[s + 4]) for s in range(4)]
        else:
            even = odd = parts
        even, odd = four(even, -1), four([eighth(odd[s], s, -1) for s in range(4)], -1)
        for r in range(TILES):
            value = (odd if r % 2 else even)[r // 2]
            if r:
                value = times(value, step(page_ref, plain, r))
            for part in range(2):
                at = rows, slice(part * LANES, (part + 1) * LANES)
                high_ref[r, *at], low_ref[r, *at] = split(value[part])


def filter_kernel(
    me_ref, pages, matrices, p0, p1, p2, p3, out_ref, page_ref, matrix_ref, sem_ref, held_ref, x_ref, f_ref, high_ref, low_ref
):
    me = me_ref[0]
    pieces = [(piece, held_ref.at[mask]) for mask, piece in enumerate((p0, p1, p2, p3))]
    loads = Loads(sem_ref, [(pages.at[me], page_ref), (matrices, matrix_ref), *pieces])
    for mask in range(GROUP):
        loads.wait(2 + mask)
        at = (me ^ mask) * 8
        for a in range(16):
            for tile in range(TILES):
                rows = pl.ds(pl.multiple_of(a * 32 + at, 8), 8)
                x_ref[tile, rows, :] = held_ref[mask, pl.ds(a * 64 + tile, 8, stride=8), :]
    loads.wait(0, 1)
    outer_transform(x_ref, TILES, 0, page_ref, MIX, matrix_ref, 1, f_ref, high_ref, low_ref)
    inner_transform(f_ref, TILES, 1, 0, page_ref, high_ref, low_ref)
    for r in range(TILES):
        out_ref[r] = right_product(matrix_ref, 0, high_ref[r], low_ref[r])


def drive_outer_kernel(
    me_ref,
    pages,
    matrices,
    own_ref,
    spectrum,
    mine_ref,
    other_ref,
    page_ref,
    matrix_ref,
    filter_ref,
    mix_ref,
    ahead_ref,
    sem_ref,
    x_ref,
    high_ref,
    low_ref,
):
    page = pages.at[me_ref[0]]
    first = [(page.at[pl.ds(MIX, 2 * LANES)], mix_ref), (matrices.at[pl.ds(2, 2)], ahead_ref)]
    tables_here = Loads(sem_ref.at[pl.ds(0, 2)], first)
    for half in range(2):
        x_ref[half] = own_ref[pl.ds(half, ROWS, stride=2), :]
    tables_here.wait(0, 1)
    loads = Loads(sem_ref.at[pl.ds(2, 3)], [(page, page_ref), (matrices, matrix_ref), (spectrum, filter_ref)])
    outer_transform(x_ref, 2, 1, mix_ref, 0, ahead_ref, 0, other_ref, high_ref, low_ref)
    outer_transform(x_ref, 2, 0, mix_ref, 0, ahead_ref, 0, mine_ref, high_ref, low_ref)
    loads.wait(0, 1, 2)


def product_kernel(
    me_ref,
    own_ref,
    peer_ref,
    page_ref,
    matrix_ref,
    filter_ref,
    other_ref,
    left_high_ref,
    left_low_ref,
    f_ref,
    d_ref,
    high_ref,
    low_ref,
):
    core = me_ref[0] & 1
    for which, piece_ref in ((core, own_ref), (1 - core, peer_ref)):
        for half in range(2):
            f_ref[2 * which + half] = piece_ref[half]
    inner_transform(f_ref, 4, 0, 16, page_ref, high_ref, low_ref)
    for r in range(TILES):
        x, h = right_product(matrix_ref, 0, high_ref[r], low_ref[r]), filter_ref[r]
        value = times((x[:, :LANES], x[:, LANES:]), (h[:, :LANES], h[:, LANES:]))
        d_ref[r] = right_product(matrix_ref, 1, *split(jnp.concatenate(value, 1)))
    for chunk in range(Q // CHUNK):
        rows = slice(chunk * CHUNK, (chunk + 1) * CHUNK)
        q, kappa = divmod(chunk * CHUNK, LANES)
        angle = turn(page_ref, rows)
        parts = []
        for r in range(TILES):
            value = d_ref[r, rows, :LANES], d_ref[r, rows, LANES:]
            if r:
                value = times(value, step(page_ref, 1, r), True)
            parts.append(value)
        even, odd = four(parts[0::2], 1), four(parts[1::2], 1)
        odd = [eighth(odd[s], s, 1) for s in range(4)]
        for s in range(TILES):
            value = (minus if s >= 4 else plus)(even[s % 4], odd[s % 4])
            value = times(times(value, angle, True), column(page_ref, rows, 2 * s), True)
            for part in range(2):
                at = slice(part * LANES + kappa, part * LANES + kappa + CHUNK), slice(q * LANES, (q + 1) * LANES)
                high_ref[s, *at], low_ref[s, *at] = split(value[part])
    for t in range(4):
        left_high_ref[t] = high_ref[4 * core + t]
        left_low_ref[t] = low_ref[4 * core + t]
        high, low = high_ref[4 * (1 - core) + t], low_ref[4 * (1 - core) + t]
        d_ref[t] = left_product(matrix_ref, 0, high, low)
    blend(d_ref, page_ref, other_ref)


def blend(d_ref, page_ref, out_ref):
    for chunk in range(LANES // CHUNK):
        rows = slice(chunk * CHUNK, (chunk + 1) * CHUNK)
        mix = mixes(page_ref, 0, rows, 16)
        for t in range(4):
            v = [
                d_ref[t, part * LANES + rows.start : part * LANES + rows.stop, q * LANES : (q + 1) * LANES]
                for q in range(2)
                for part in range(2)
            ]
            for a in range(4):
                value = mixed(mix[4 * a : 4 * a + 4], v)
                out_ref[pl.ds((a * LANES + rows.start) * 4 + t, CHUNK, stride=4), :] = value


def mine_kernel(high_ref, low_ref, page_ref, matrix_ref, out_ref, d_ref):
    for t in range(4):
        d_ref[t] = left_product(matrix_ref, 0, high_ref[t], low_ref[t])
    blend(d_ref, page_ref, out_ref)


VMEM_LIMIT = 32 * 1024 * 1024
VMEM_ALL = 60 * 1024 * 1024
FILTER_FLOPS = 3 * 2 * 256 * 256 * 256 * 16


def whole(s):
    return pl.BlockSpec(s.shape, lambda *_, n=len(s.shape): (0,) * n)


def call(kernel, out_shapes, args, in_specs=None, scratch=(), prefetch=0, flops=0, limit=VMEM_LIMIT, out_specs=None):
    nbytes = sum(a.size * a.dtype.itemsize for a in args) + sum(int(np.prod(s.shape)) * 4 for s in out_shapes)
    single = len(out_shapes) == 1
    out_specs = out_specs or [whole(s) for s in out_shapes]
    return pl.pallas_call(
        kernel,
        out_shape=out_shapes[0] if single else out_shapes,
        grid_spec=pltpu.PrefetchScalarGridSpec(
            num_scalar_prefetch=prefetch,
            grid=(1,),
            in_specs=in_specs or [whole(a) for a in args[prefetch:]],
            out_specs=out_specs[0] if single else out_specs,
            scratch_shapes=list(scratch),
        ),
        compiler_params=pltpu.CompilerParams(vmem_limit_bytes=limit),
        cost_estimate=pl.CostEstimate(flops=flops, bytes_accessed=nbytes, transcendentals=0),
    )(*args)


def shape(*dims):
    return jax.ShapeDtypeStruct(dims, F32)


HBM = pl.BlockSpec(memory_space=pltpu.HBM)


def stay(x):
    return pltpu.with_memory_space_constraint(x, pltpu.HBM)


def work(count):
    return [pltpu.VMEM((count, Q, Q), BF)] * 2


def tie_kernel(rows_ref, _, out_ref):
    pass


def after(rows, other):
    return pl.pallas_call(
        tie_kernel,
        out_shape=shape(*rows.shape),
        grid=(1,),
        in_specs=[pl.BlockSpec(memory_space=pl.ANY), whole(other)],
        out_specs=pl.BlockSpec(memory_space=pl.ANY),
        input_output_aliases={0: 0},
        compiler_params=pltpu.CompilerParams(vmem_limit_bytes=VMEM_LIMIT),
    )(rows, other)


def across(rows, mask):
    size = lax.axis_size("seq")
    return lax.ppermute(rows, "seq", [(i, i ^ mask) for i in range(size)])


def local(queries, keys, values, short_taps, long_filter, skip_gain):
    everyone = ("seq", "chan")
    size = lax.axis_size(everyone)
    seq_size = lax.axis_size("seq")
    me = (lax.axis_index("seq") % GROUP).astype(jnp.int32).reshape(1)
    channels = queries.shape[0]

    held = [pltpu.VMEM((4, 16, 2 * COLS), F32), pltpu.VMEM((4, 2 * LANES, LANES), F32), pltpu.SemaphoreType.DMA((8,))]
    filter_rows = call(pack_filter_kernel, [shape(16, 64, LANES)], (long_filter,), [HBM], held, limit=VMEM_ALL, out_specs=[HBM])
    alike = [list(range(member, seq_size, GROUP)) for member in range(GROUP)]
    filter_rows = lax.all_to_all(
        filter_rows, "seq", 0, 0, tiled=True, axis_index_groups=alike
    ).reshape(2 * ROWS, LANES)

    edges = jnp.stack((queries[:, -2], queries[:, -1], keys[:, -2], keys[:, -1], values[:, -2], values[:, -1]))
    before = lax.ppermute(edges, everyone, [(i, i + 1) for i in range(size - 1)])
    small = jnp.concatenate((short_taps.reshape(9, channels), skip_gain[None], before)).T
    outs = [shape(2 * ROWS, LANES), shape(channels, COLS), shape(8, 16)]
    packed, drive, token = call(drive_kernel, outs, (keys, values, small))
    filter_rows = after(filter_rows, token)
    filter_far = across(filter_rows, 2)
    own = lax.all_to_all(packed.reshape(size, -1, LANES), everyone, 0, 0, tiled=True).reshape(2 * ROWS, LANES)

    flops = 3 * 2 * 256 * 256 * 256 * 8
    pieces = tuple(map(stay, (filter_rows, across(filter_rows, 1), filter_far, across(filter_far, 1))))
    matrices, pages = (stay(jnp.asarray(t)) for t in tables())
    page, table = shape(PAGE, LANES), jax.ShapeDtypeStruct(matrices.shape, BF)
    vmem = lambda s: pltpu.VMEM(s.shape, s.dtype)
    f32 = lambda *dims: pltpu.VMEM(dims, F32)
    sems = lambda count: pltpu.SemaphoreType.DMA((count,))
    spectrum = call(
        filter_kernel,
        [shape(TILES, Q, Q)],
        (me, pages, matrices, *pieces),
        [HBM] * 6,
        [vmem(page), vmem(table), sems(6), f32(GROUP, 2 * ROWS, LANES), f32(TILES, ROWS, LANES), f32(TILES, 2, Q, LANES)]
        + work(TILES),
        1,
        FILTER_FLOPS,
        VMEM_ALL,
    )
    mine, other, *loaded = call(
        drive_outer_kernel,
        [shape(2, 2, Q, LANES), shape(2, 2, Q, LANES), page, table, shape(TILES, Q, Q)],
        (me, pages, matrices, own, stay(spectrum)),
        [HBM, HBM, whole(own), HBM],
        [f32(2 * LANES, LANES), pltpu.VMEM((2, Q, Q), BF), sems(5), f32(2, ROWS, LANES)] + work(2),
        1,
        flops,
    )
    left = jax.ShapeDtypeStruct((4, Q, Q), BF)
    page, table, _ = loaded
    other, *left = call(
        product_kernel,
        [shape(4 * ROWS, LANES), left, left],
        (me, mine, across(other, 1), *loaded),
        None,
        [f32(4, 2, Q, LANES), f32(TILES, Q, Q)] + work(TILES),
        1,
        3 * flops,
    )
    mine = call(mine_kernel, [shape(4 * ROWS, LANES)], (*left, page, table), None, [f32(4, Q, Q)], 0, flops)
    result = mine + across(other, 1)
    gain, direct = call(gate_kernel, [shape(channels, COLS)] * 2, (queries, drive, small))
    returned = lax.all_to_all(result.reshape(size, -1, LANES), everyone, 0, 0, tiled=True).reshape(4 * ROWS, LANES)
    return call(finish_kernel, [shape(channels, COLS)], (returned, gain, direct))


def solution(mesh):
    spread = P(None, ("seq", "chan"))
    in_specs = (spread, spread, spread, P(), P("chan", "seq"), P())
    return jax.shard_map(local, mesh=mesh, in_specs=in_specs, out_specs=spread, check_vma=False)
```
